128 devices in a mesh: dp: 8 (over x, core), ctx: 16 (over y, z).
Axes of the slice: x: 4, y: 4, z: 4, core: 2. Of those that a mesh axis runs over, the one named last changes fastest.
Arguments:
- queries: bfloat16 [16384, 4096], P(('dp', 'ctx')), may hold values from -2.5 to 2.5
- keys: bfloat16 [16384, 512], P(('dp', 'ctx')), may hold values from -2.5 to 2.5
- values: bfloat16 [16384, 512], P(('dp', 'ctx')), may hold values from -4 to 4
- attn_out: bfloat16 [16384, 4096], P(('dp', 'ctx')), may hold values from -3 to 3
- out_grad: bfloat16 [16384, 4096], P(('dp', 'ctx')), may hold values from -4 to 4
- send_slot: int32 [128, 128], P(('dp', 'ctx')), may hold values from 0 to 127, each once within a row
- proof_length_list: int32 [8, 4], P('dp'), may hold values from 1 to 1024, 2048 in all within a row
Outputs:
- q_grad: bfloat16 [16384, 4096], P(('dp', 'ctx'))
- k_grad: bfloat16 [16384, 512], P(('dp', 'ctx'))
- v_grad: bfloat16 [16384, 512], P(('dp', 'ctx'))
The draws below stay inside these ranges and needn't reach their ends.
Inputs may be any that keep to these rules, and one draw needn't show every extreme that they name: `send_slot`: each row holds every value of 0 to 127 once. `proof_length_list`: each pack's lengths sum to 2048.
All inputs are finite; a program needn't handle non-finite values.
Results may differ from the reference program's by a relative error of at most 0.0049.
Values may be sent and summed in bfloat16 or wider, within the bound.
No kernel may reach another device: no remote copies, remote signals or barrier semaphores. Data moves between devices by JAX's collectives and lax.ppermute only.
A program may use at most 128 MiB of HBM per device.

```python
import math
import jax
import jax.numpy as jnp
import numpy as np
from jax import lax

HEADS = 32
KV_HEADS = 4
HEAD_DIM = 128
TOK_DEV = 128
DOCS = 4
SOURCES = 128
GROUPS = 8
GROUP_TOKENS = 2048
TOKENS = 16384
N_DP = 8
N_CTX = 16


def levels(key, shape, pieces, low, top_value):
    loudness, own = 1.0, jax.random.fold_in(key, 6)
    for dim, blocks in pieces:
        steps = jnp.exp(jax.random.uniform(jax.random.fold_in(own, dim), (blocks,), jnp.float32, low / len(pieces), top_value / len(pieces)))
        loudness = loudness * jnp.repeat(steps, shape[dim] // blocks).reshape([-1 if axis == dim else 1 for axis in range(len(shape))])
    return loudness


def split_up(amount, total, bound, slope):
    portions = [(1 << 20) // math.isqrt(grade ** slope) + 1 for grade in range(2, amount + 1)]
    surplus, counts = total - bound - (amount - 1), [1] * (amount - 1)
    while surplus > 0:
        free = [i for i in range(amount - 1) if counts[i] < bound]
        mass, left = sum([portions[i] for i in free]), surplus
        for i in free:
            addition = min(bound - counts[i], max(1, left * portions[i] // mass), surplus)
            counts[i] = counts[i] + addition
            surplus = surplus - addition
    return np.array([bound] + counts)


def uneven_parts(rng, amount, total, bound, skew):
    if amount == 2:
        one = jax.random.randint(rng, (), max(1, total - bound), min(bound, total - 1) + 1)
        return jnp.stack([one, total - one])
    tallies = jnp.asarray(split_up(amount, total, bound, skew), jnp.int32)
    twos = (amount - 1) // 2
    giver, sink = tallies[1:1 + 2 * twos:2], tallies[2:2 + 2 * twos:2]
    slack = jnp.minimum(giver - 1, bound - sink)
    shifted = jax.random.randint(jax.random.fold_in(rng, 1), (twos,), 0, 1 << 20) % (slack + 1)
    tallies = tallies.at[1:1 + 2 * twos:2].set(giver - shifted).at[2:2 + 2 * twos:2].set(sink + shifted)
    return tallies[jax.random.permutation(jax.random.fold_in(rng, 2), amount)]


def centred(key, dims, width, reach, shards=(), kind=jnp.bfloat16):
    values = width * jax.random.normal(key, dims, jnp.float32)
    if shards:
        values = values * levels(key, dims, shards, -0.22, 0.18)
    return jnp.clip(values, -reach, reach).astype(kind)


def setup_inputs(seed: int = 0) -> dict:
    splits = jax.random.split(jax.random.key(seed), 8)
    queries = centred(splits[0], (TOKENS, HEADS * HEAD_DIM), 1.0, 2.5, ((0, 128),))
    keys = centred(splits[1], (TOKENS, KV_HEADS * HEAD_DIM), 1.0, 2.5, ((0, 128),))
    values = centred(splits[2], (TOKENS, KV_HEADS * HEAD_DIM), 1.0, 4.0, ((0, 128),))
    attn_out = centred(splits[3], (TOKENS, HEADS * HEAD_DIM), 0.5, 3.0, ((0, 128),))
    out_grad = centred(splits[4], (TOKENS, HEADS * HEAD_DIM), 1.0, 4.0, ((0, 128),))
    send_slot = jax.vmap(lambda own: jax.random.permutation(own, TOK_DEV))(jax.random.split(splits[5], SOURCES)).reshape((SOURCES, TOK_DEV)).astype(jnp.int32)
    proof_length_list = jax.vmap(lambda own: uneven_parts(own, DOCS, GROUP_TOKENS, GROUP_TOKENS // 2, 1))(jax.random.split(splits[6], GROUPS)).reshape((GROUPS, DOCS)).astype(jnp.int32)
    return dict(queries=queries, keys=keys, values=values, attn_out=attn_out, out_grad=out_grad, send_slot=send_slot, proof_length_list=proof_length_list)


def fold_position(index, rows, half, count):
    return jnp.where(rows < half, index * half + rows, (2 * count - 1 - index) * half + rows - half)


def doc_start(token_locations, lengths):
    ends = jnp.cumsum(lengths)
    return jnp.sum(jnp.where(ends[None, :] <= token_locations[:, None], lengths[None, :], 0), axis=1).astype(jnp.int32)


def query_head_group(query_matrix, key_matrix, value_matrix, output_matrix, gradient_matrix, token_locations, proof_begins):
    scale = HEAD_DIM ** -0.5
    qf = query_matrix.astype(jnp.float32)
    kf = key_matrix.astype(jnp.float32)
    value_float = value_matrix.astype(jnp.float32)
    gf = gradient_matrix.astype(jnp.float32)
    scores = jnp.einsum("qme,ke->mqk", qf, kf) * scale
    allowed = (token_locations[None, :] <= token_locations[:, None]) & (token_locations[None, :] >= proof_begins[:, None])
    total = jnp.sum(jnp.exp(jnp.where(allowed[None], scores, -jnp.inf)), axis=-1)
    log_sum_exponent = jnp.log(total)
    output_grad_dot = jnp.sum(output_matrix.astype(jnp.float32) * gf, axis=-1).T
    probs = jnp.exp(jnp.where(allowed[None], scores - log_sum_exponent[..., None], -jnp.inf))
    probs_low = lax.optimization_barrier(probs.astype(jnp.bfloat16)).astype(jnp.float32)
    value_gradient = jnp.einsum("mqk,qme->ke", probs_low, gf)
    probability_gradient = jnp.einsum("qme,ke->mqk", gf, value_float)
    dscores = lax.optimization_barrier((probs * (probability_gradient - output_grad_dot[..., None])).astype(jnp.bfloat16)).astype(jnp.float32)
    query_gradient = jnp.einsum("mqk,ke->qme", dscores, kf) * scale
    key_gradient = jnp.einsum("mqk,qme->ke", dscores, qf) * scale
    return query_gradient, key_gradient, value_gradient


def reference(queries, keys, values, attn_out, out_grad, send_slot, proof_length_list):
    devices = N_DP * N_CTX
    share = TOK_DEV // devices
    half = TOK_DEV // 2
    members = HEADS // KV_HEADS
    row = jnp.arange(TOKENS, dtype=jnp.int32)
    source = row // TOK_DEV
    slot = send_slot.reshape(TOKENS).astype(jnp.int32)
    target = slot // share
    local = source * share + slot % share
    dest = ((target // N_CTX) * GROUP_TOKENS + fold_position(target % N_CTX, local, half, N_CTX)).astype(jnp.int32)

    def arranged_rows(array):
        return jnp.zeros_like(array).at[dest].set(array)

    wide_shape = (N_DP, GROUP_TOKENS, KV_HEADS, members, HEAD_DIM)
    slim_layout = (N_DP, GROUP_TOKENS, KV_HEADS, HEAD_DIM)
    query_bundle = arranged_rows(queries).reshape(wide_shape).transpose(0, 2, 1, 3, 4)
    output_bundle = arranged_rows(attn_out).reshape(wide_shape).transpose(0, 2, 1, 3, 4)
    gradient_bundle = arranged_rows(out_grad).reshape(wide_shape).transpose(0, 2, 1, 3, 4)
    key_bundle = arranged_rows(keys).reshape(slim_layout).transpose(0, 2, 1, 3)
    value_bundle = arranged_rows(values).reshape(slim_layout).transpose(0, 2, 1, 3)

    def single_bundle(inputs):
        qgrp, kgrp, vgrp, ogrp, ggrp, lengths = inputs
        token_locations = jnp.arange(GROUP_TOKENS, dtype=jnp.int32)
        proof_begins = doc_start(token_locations, lengths.astype(jnp.int32))

        def one_head(parts):
            return query_head_group(parts[0], parts[1], parts[2], parts[3], parts[4], token_locations, proof_begins)

        return lax.map(one_head, (qgrp, kgrp, vgrp, ogrp, ggrp))

    query_gradient, key_gradient, value_gradient = lax.map(single_bundle, (query_bundle, key_bundle, value_bundle, output_bundle, gradient_bundle, proof_length_list))
    query_gradient = query_gradient.transpose(0, 2, 1, 3, 4).reshape(TOKENS, HEADS * HEAD_DIM)
    key_gradient = key_gradient.transpose(0, 2, 1, 3).reshape(TOKENS, KV_HEADS * HEAD_DIM)
    value_gradient = value_gradient.transpose(0, 2, 1, 3).reshape(TOKENS, KV_HEADS * HEAD_DIM)
    return (query_gradient[dest].astype(jnp.bfloat16), key_gradient[dest].astype(jnp.bfloat16), value_gradient[dest].astype(jnp.bfloat16))
```

```python
import jax
import jax.numpy as jnp
from jax import lax
from jax.experimental import pallas as pl
from jax.experimental.pallas import tpu as pltpu
from jax.sharding import PartitionSpec as P

D = 128
ROWS = 128
TILE = 256
TOKENS = 2048
TILES = TOKENS // TILE
SCALE = D ** (-0.5)
LOG2E = 1.4426950408889634
VMEM = 56 * 1024 * 1024
NT = (((1,), (1,)), ((), ()))
NN = (((1,), (0,)), ((), ()))


def dot(a, b, dims=NN):
    return lax.dot_general(a, b, dims, preferred_element_type=jnp.float32)


def plan_matrix(slot_ref):
    p = lax.broadcasted_iota(jnp.int32, (ROWS, ROWS), 0)
    return (p == slot_ref[...]).astype(jnp.float32)


def pack_kernel(slot_ref, q_ref, o_ref, g_ref, k_ref, v_ref, out_ref):
    plan = plan_matrix(slot_ref).astype(jnp.bfloat16)

    def placed(columns):
        return dot(plan, columns).astype(jnp.bfloat16).reshape(4, 2, 16, D)

    lane = lax.broadcasted_iota(jnp.int32, (ROWS, D), 1)
    delta = jnp.zeros((ROWS, D), jnp.float32)
    for head in range(8):
        high, core, h = head // 4, (head // 2) % 2, head % 2
        cols = slice(head * D, (head + 1) * D)
        g = g_ref[:, cols]
        out_ref[:, core, :, 0, high, h * 16 : h * 16 + 16, :] = placed(q_ref[:, cols])
        out_ref[:, core, :, 0, high, 32 + h * 16 : 48 + h * 16, :] = placed(g)
        total = jnp.sum(
            o_ref[:, cols].astype(jnp.float32) * g.astype(jnp.float32), axis=1, keepdims=True
        )
        delta = jnp.where(lane == head, total, delta)
    first = delta.astype(jnp.bfloat16).astype(jnp.float32)
    second = (delta - first).astype(jnp.bfloat16).astype(jnp.float32)
    third = delta - first - second
    parts = first + pltpu.roll(second, 8, 1) + pltpu.roll(third, 16, 1)
    parts = placed(parts.astype(jnp.bfloat16))
    k = placed(k_ref[...])
    v = placed(v_ref[...])
    for high in range(2):
        out_ref[:, 0, :, 0, high, 64:80, :] = k
        out_ref[:, 1, :, 0, high, 64:80, :] = v
        for core in range(2):
            out_ref[:, core, :, 0, high, 80:96, :] = parts


def swap_matrix():
    r = lax.broadcasted_iota(jnp.int32, (256, 256), 0)
    c = lax.broadcasted_iota(jnp.int32, (256, 256), 1)
    same = ((r >> 4) == (c & 15)) & ((r & 15) == (c >> 4))
    return same.astype(jnp.float32).astype(jnp.bfloat16)


def attention_kernel(
    info_ref, recv_ref, other_ref, back_ref, give_ref,
    qs, gs, ks, vs, kt, dt, es, dks, dvs, dqs,
):
    core = info_ref[0]
    pair = info_ref[1]
    end0 = info_ref[2]
    end1 = end0 + info_ref[3]
    end2 = end1 + info_ref[4]

    def begin(at):
        return jnp.where(
            at >= end2, end2, jnp.where(at >= end1, end1, jnp.where(at >= end0, end0, 0))
        )

    swap = swap_matrix()
    pieces = [(half, part) for half in range(2) for part in range(4)]

    def places(half, part):
        for c in range(16):
            at = (c if half == 0 else 31 - c) * 64 + part * 16
            yield c, at // TILE, at % TILE, at

    row = lax.broadcasted_iota(jnp.int32, (16, D), 0)
    lane = lax.broadcasted_iota(jnp.int32, (16, D), 1)
    pick = ((lane & 7) == pair * 2 + row) & (lane < 24) & (row < 2)
    pick = pick.astype(jnp.float32).astype(jnp.bfloat16)

    for half, part in pieces:
        src = slice(half * 64 + part * 16, half * 64 + part * 16 + 16)

        def rows(n):
            return recv_ref[src, n * 16 : n * 16 + 16, :].reshape(256, D)

        def sorted_pair(a, b):
            return dot(swap, jnp.concatenate([a, b], axis=1)).astype(jnp.bfloat16)

        q = sorted_pair(rows(0), rows(1))
        g = sorted_pair(rows(2), rows(3))
        mine = rows(4)
        other = other_ref[src].reshape(256, D)
        k = jnp.where(core == 0, mine, other)
        v = jnp.where(core == 0, other, mine)
        kv = sorted_pair(k, v)
        d = dot(swap, rows(5)).astype(jnp.bfloat16)
        for c, tile, off, at in places(half, part):
            r = slice(c * 16, c * 16 + 16)
            qs[tile, off : off + 16, :] = q[r, :D]
            qs[tile, TILE + off : TILE + off + 16, :] = q[r, D:]
            gs[tile, off : off + 16, :] = g[r, :D]
            gs[tile, TILE + off : TILE + off + 16, :] = g[r, D:]
            ks[tile, off : off + 16, :] = kv[r, :D]
            vs[tile, off : off + 16, :] = kv[r, D:]
            dqs[tile, off : off + 16, :] = d[r]

    ident = (
        lax.broadcasted_iota(jnp.int32, (D, D), 0) == lax.broadcasted_iota(jnp.int32, (D, D), 1)
    ).astype(jnp.float32).astype(jnp.bfloat16)
    for tile in range(TILES):
        kt[tile] = dot(ident, ks[tile], NT).astype(jnp.bfloat16)
        dt[tile] = dot(pick, dqs[tile, :TILE, :], NT)[:8]
    dks[...] = jnp.zeros_like(dks)
    dvs[...] = jnp.zeros_like(dvs)

    key_row = lax.broadcasted_iota(jnp.int32, (TILE, TILE), 0)
    query_lane = lax.broadcasted_iota(jnp.int32, (1, TILE), 1)

    def query_tile(i, carry):
        start = begin(i * TILE)
        first = start // TILE
        q = qs[i]
        g = gs[i]
        at = i * TILE + query_lane
        from_ = begin(at)

        def scores(j, total):
            s = dot(ks[j], q, NT)
            key = key_row + j * TILE
            seen = (key <= at) & (key >= from_)
            e = jnp.exp2(s * (SCALE * LOG2E))
            e = jnp.concatenate(
                [jnp.where(seen, e[:, :TILE], 0.0), jnp.where(seen, e[:, TILE:], 0.0)], axis=1
            )
            es[j - first] = e
            return total + jnp.sum(e.reshape(TILE // 8, 8, 2 * TILE), axis=0)

        total = lax.fori_loop(first, i + 1, scores, jnp.zeros((8, 2 * TILE), jnp.float32))
        inverse = 1.0 / jnp.sum(total, axis=0, keepdims=True)
        delta = jnp.concatenate([dt[i, 0:1, :], dt[i, 1:2, :]], axis=1)

        def grads(j, acc):
            p = es[j - first] * inverse
            dp = dot(vs[j], g, NT)
            ds = (p * (dp - delta)).astype(jnp.bfloat16)
            dvs[j] += dot(p.astype(jnp.bfloat16), g)
            dks[j] += dot(ds, q)
            return acc + dot(kt[j], ds)

        dq = lax.fori_loop(first, i + 1, grads, jnp.zeros((D, 2 * TILE), jnp.float32))
        dqs[i] = jnp.transpose(dq * SCALE).astype(jnp.bfloat16)
        return carry

    lax.fori_loop(0, TILES, query_tile, 0)

    for half, part in pieces:
        src = slice(half * 64 + part * 16, half * 64 + part * 16 + 16)
        dq0, dq1, mine, other = [], [], [], []
        for c, tile, off, at in places(half, part):
            dq0.append(dqs[tile, off : off + 16, :])
            dq1.append(dqs[tile, TILE + off : TILE + off + 16, :])
            dk = dks[tile, off : off + 16, :] * SCALE
            dv = dvs[tile, off : off + 16, :]
            mine.append(jnp.where(core == 0, dk, dv).astype(jnp.bfloat16))
            other.append(jnp.where(core == 0, dv, dk).astype(jnp.bfloat16))

        def unsorted_pair(a, b):
            both = jnp.concatenate(
                [jnp.concatenate(a, axis=0), jnp.concatenate(b, axis=0)], axis=1
            )
            both = dot(swap, both).astype(jnp.bfloat16)
            return both[:, :D].reshape(16, 16, D), both[:, D:].reshape(16, 16, D)

        a, b = unsorted_pair(dq0, dq1)
        back_ref[src, 0:16, :] = a
        back_ref[src, 16:32, :] = b
        a, b = unsorted_pair(mine, other)
        back_ref[src, 32:48, :] = a
        give_ref[src] = b


def unpack_kernel(slot_ref, back_ref, q_ref, k_ref, v_ref):
    plan = jnp.transpose(plan_matrix(slot_ref)).astype(jnp.bfloat16)
    for head in range(8):
        high, core, h = head // 4, (head // 2) % 2, head % 2
        rows = back_ref[:, core, :, 0, high, h * 16 : h * 16 + 16, :].reshape(ROWS, D)
        q_ref[:, head * D : (head + 1) * D] = dot(plan, rows).astype(jnp.bfloat16)
    both = jnp.concatenate([plan, plan], axis=1)
    for core, out in ((0, k_ref), (1, v_ref)):
        rows = jnp.concatenate(
            [back_ref[:, core, :, 0, high, 32:48, :].reshape(ROWS, D) for high in range(2)], axis=0
        )
        out[...] = dot(both, rows).astype(jnp.bfloat16)


def swapped(array):
    return lax.ppermute(array, "dp", [(i, i ^ 1) for i in range(8)])


def per_device(queries, keys, values, attn_out, out_grad, send_slot, proof_length_list):
    core = lax.axis_index("dp") % 2
    ctx = lax.axis_index("ctx")
    lengths = proof_length_list[0]
    lengths = jnp.where(ctx // 8 == core, lengths, swapped(lengths))
    info = jnp.concatenate([jnp.stack([core, (ctx % 2) * 2 + core]).astype(jnp.int32), lengths])
    params = pltpu.CompilerParams(vmem_limit_bytes=VMEM)

    whole = pl.BlockSpec((1, ROWS), lambda b: (0, 0))
    wide = pl.BlockSpec((ROWS, 8 * D), lambda b: (0, b))
    slim = pl.BlockSpec((ROWS, D), lambda b: (0, b))
    cut = (4, 2, 2, 4, 2)

    def blocks(rows):
        return pl.BlockSpec((4, 2, 2, 1, 2, rows, D), lambda b: (0, 0, 0, b, 0, 0, 0))

    send = pl.pallas_call(
        pack_kernel,
        grid=(4,),
        in_specs=[whole, wide, wide, wide, slim, slim],
        out_specs=blocks(96),
        out_shape=jax.ShapeDtypeStruct((*cut, 96, D), jnp.bfloat16),
        compiler_params=params,
        name="pack",
    )(send_slot, queries, attn_out, out_grad, keys, values)
    recv = lax.all_to_all(
        send.reshape(128, 96, D), ("dp", "ctx"), split_axis=0, concat_axis=0, tiled=True
    )
    other = swapped(recv[:, 64:80])

    bf, f32 = jnp.bfloat16, jnp.float32
    back, give = pl.pallas_call(
        attention_kernel,
        in_specs=[
            pl.BlockSpec(memory_space=pltpu.SMEM),
            pl.BlockSpec(memory_space=pltpu.VMEM),
            pl.BlockSpec(memory_space=pltpu.VMEM),
        ],
        out_specs=[pl.BlockSpec(memory_space=pltpu.VMEM)] * 2,
        out_shape=[
            jax.ShapeDtypeStruct((128, 48, D), bf),
            jax.ShapeDtypeStruct((128, 16, D), bf),
        ],
        scratch_shapes=[
            pltpu.VMEM((TILES, 2 * TILE, D), bf),
            pltpu.VMEM((TILES, 2 * TILE, D), bf),
            pltpu.VMEM((TILES, TILE, D), bf),
            pltpu.VMEM((TILES, TILE, D), bf),
            pltpu.VMEM((TILES, D, TILE), bf),
            pltpu.VMEM((TILES, 8, TILE), f32),
            pltpu.VMEM((TILES, TILE, 2 * TILE), f32),
            pltpu.VMEM((TILES, TILE, D), f32),
            pltpu.VMEM((TILES, TILE, D), f32),
            pltpu.VMEM((TILES, 2 * TILE, D), bf),
        ],
        compiler_params=params,
        name="attention",
    )(info, recv, other)
    back = back.at[:, 32:48].add(swapped(give))
    back = lax.all_to_all(back, ("dp", "ctx"), split_axis=0, concat_axis=0, tiled=True)
    return pl.pallas_call(
        unpack_kernel,
        grid=(4,),
        in_specs=[whole, blocks(48)],
        out_specs=[wide, slim, slim],
        out_shape=[
            jax.ShapeDtypeStruct((ROWS, 32 * D), bf),
            jax.ShapeDtypeStruct((ROWS, 4 * D), bf),
            jax.ShapeDtypeStruct((ROWS, 4 * D), bf),
        ],
        compiler_params=params,
        name="unpack",
    )(send_slot, back.reshape(*cut, 48, D))


def solution(mesh):
    rows = P(("dp", "ctx"), None)
    return jax.shard_map(
        per_device,
        mesh=mesh,
        in_specs=(rows, rows, rows, rows, rows, rows, P("dp", None)),
        out_specs=(rows, rows, rows),
        check_vma=False,
    )
```

```python
import jax
import jax.numpy as jnp
from jax import lax
from jax.experimental import pallas as pl
from jax.experimental.pallas import tpu as pltpu
from jax.sharding import PartitionSpec as P

D = 128
ROWS = 128
KEYS = 256
QUERIES = 256
TOKENS = 2048
KTILES = TOKENS // KEYS
QTILES = TOKENS // QUERIES
UNROLL = 6
CUT = (4, 2, 2, 4, 2)
SCALE = D ** (-0.5)
LOG2E = 1.4426950408889634
VMEM = 32 * 1024 * 1024
NT = (((1,), (1,)), ((), ()))
NN = (((1,), (0,)), ((), ()))


def dot(a, b, dims=NN):
    return lax.dot_general(a, b, dims, preferred_element_type=jnp.float32)


def plan_matrix(slot_ref):
    p = lax.broadcasted_iota(jnp.int32, (ROWS, ROWS), 0)
    return (p == slot_ref[...]).astype(jnp.float32)


def pack_kernel(
    slot_ref, q_hbm, o_hbm, g_hbm, k_hbm, v_hbm, out_ref, qs, os, gs, ks, vs, arrived
):
    copies = []
    for b in range(4):
        cols = pl.ds(b * 8 * D, 8 * D)
        for n, (far, near) in enumerate(((q_hbm, qs), (g_hbm, gs), (o_hbm, os))):
            copies.append(
                pltpu.make_async_copy(far.at[:, cols], near.at[b], arrived.at[b * 3 + n])
            )
    copies.append(pltpu.make_async_copy(k_hbm, ks, arrived.at[12]))
    copies.append(pltpu.make_async_copy(v_hbm, vs, arrived.at[13]))
    for copy in copies:
        copy.start()
    plan = plan_matrix(slot_ref).astype(jnp.bfloat16)
    lane = lax.broadcasted_iota(jnp.int32, (ROWS, D), 1)

    def placed(columns):
        return dot(plan, columns).astype(jnp.bfloat16).reshape(4, 2, 16, D)

    for b in range(4):
        for copy in copies[b * 3 : b * 3 + 3]:
            copy.wait()
        delta = jnp.zeros((ROWS, D), jnp.float32)
        for head in range(8):
            high, core, h = head // 4, (head // 2) % 2, head % 2
            cols = slice(head * D, (head + 1) * D)
            g = gs[b, :, cols]
            out_ref[:, core, :, b, high, h * 16 : h * 16 + 16, :] = placed(qs[b, :, cols])
            out_ref[:, core, :, b, high, 32 + h * 16 : 48 + h * 16, :] = placed(g)
            total = jnp.sum(
                os[b, :, cols].astype(jnp.float32) * g.astype(jnp.float32), axis=1, keepdims=True
            )
            delta = jnp.where(lane == head, total, delta)
        first = delta.astype(jnp.bfloat16).astype(jnp.float32)
        second = (delta - first).astype(jnp.bfloat16).astype(jnp.float32)
        third = delta - first - second
        parts = first + pltpu.roll(second, 8, 1) + pltpu.roll(third, 16, 1)
        parts = dot(plan, parts.astype(jnp.bfloat16)).reshape(8, 16, D)
        parts = (parts[:, :8] + pltpu.roll(parts[:, 8:], 64, 2)).astype(jnp.bfloat16)
        parts = parts.reshape(4, 2, 8, D)
        for high in range(2):
            for core in range(2):
                out_ref[:, core, :, b, high, 80:88, :] = parts
    copies[12].wait()
    copies[13].wait()
    for b in range(4):
        cols = slice(b * D, (b + 1) * D)
        for core, rows in ((0, ks), (1, vs)):
            rows = placed(rows[:, cols])
            for high in range(2):
                out_ref[:, core, :, b, high, 64:80, :] = rows


def swap_matrix(bits):
    size = 16 << bits
    r = lax.broadcasted_iota(jnp.int32, (size, size), 0)
    c = lax.broadcasted_iota(jnp.int32, (size, size), 1)
    same = ((r >> 4) == (c & ((1 << bits) - 1))) & ((r & 15) == (c >> bits))
    return same.astype(jnp.float32).astype(jnp.bfloat16)


def pieces():
    for half in range(2):
        for part in range(4):
            first = half * 64 + part * 16
            yield (
                slice(first, first + 16),
                [(c if half == 0 else 31 - c) * 64 + part * 16 for c in range(16)],
            )


def take_kernel(recv_ref, out_ref):
    out_ref[...] = recv_ref[...]


def sort_kernel(info_ref, recv_ref, qs, gs, dt, ds):
    swap = swap_matrix(4)
    short = swap_matrix(3)
    for src, places in pieces():

        def rows(n):
            return recv_ref[src, n * 16 : n * 16 + 16, :].reshape(256, D)

        for n, out in ((0, qs), (2, gs)):
            both = jnp.concatenate([rows(n), rows(n + 1)], axis=1)
            both = dot(swap, both).astype(jnp.bfloat16)
            for c, at in enumerate(places):
                tile, off = at // QUERIES, at % QUERIES
                r = slice(c * 16, c * 16 + 16)
                out[tile, off : off + 16, :] = both[r, :D]
                out[tile, QUERIES + off : QUERIES + off + 16, :] = both[r, D:]
        d = recv_ref[src, 80:88, :].reshape(128, D)
        d = dot(short, d).astype(jnp.bfloat16)
        for c, at in enumerate(places):
            ds[at : at + 16, :] = d[(c % 8) * 16 : (c % 8) * 16 + 16]
    row = lax.broadcasted_iota(jnp.int32, (16, D), 0)
    lane = lax.broadcasted_iota(jnp.int32, (16, D), 1)
    pick = ((lane & 7) == info_ref[1] * 2 + row) & ((lane & 63) < 24) & (row < 2)
    for tile in range(QTILES):
        at = tile * QUERIES
        upper = int(512 <= at < 1536)
        own = (pick & (lane >> 6 == upper)).astype(jnp.float32).astype(jnp.bfloat16)
        d = dot(own, ds[at : at + QUERIES, :], NT)
        dt[tile] = jnp.concatenate([d[0:1], d[1:2]], axis=1)


def attention_kernel(
    info_ref, near_ref, far_ref, mine_ref, other_ref, qs, gs, dt, dqs, keep_ref, give_ref,
    ks, vs, kt, es, dks, dvs, dqt, sums, list_ref,
):
    core = info_ref[0]
    lengths = [jnp.where(info_ref[2] == 1, near_ref[0, n], far_ref[0, n]) for n in range(3)]
    end0 = lengths[0]
    end1 = end0 + lengths[1]
    end2 = end1 + lengths[2]

    def begin(at):
        return jnp.where(
            at >= end2, end2, jnp.where(at >= end1, end1, jnp.where(at >= end0, end0, 0))
        )

    count = jnp.int32(0)
    for i in range(QTILES):
        last = i * QUERIES // KEYS
        first = begin(jnp.int32(i * QUERIES)) // KEYS
        for j in range(last + 1):
            list_ref[0, count] = i
            list_ref[1, count] = j
            count = count + (j >= first).astype(jnp.int32)
    for extra in range(UNROLL):
        list_ref[0, count + extra] = 0
        list_ref[1, count + extra] = KTILES - 1
    trips = (count + UNROLL - 1) // UNROLL

    swap = swap_matrix(4)
    for src, places in pieces():
        mine = mine_ref[src].reshape(256, D)
        other = other_ref[src].reshape(256, D)
        both = jnp.concatenate(
            [jnp.where(core == 0, mine, other), jnp.where(core == 0, other, mine)], axis=1
        )
        both = dot(swap, both).astype(jnp.bfloat16)
        for c, at in enumerate(places):
            tile, off = at // KEYS, at % KEYS
            ks[tile, off : off + 16, :] = both[c * 16 : c * 16 + 16, :D]
            vs[tile, off : off + 16, :] = both[c * 16 : c * 16 + 16, D:]
    ident = (
        lax.broadcasted_iota(jnp.int32, (D, D), 0) == lax.broadcasted_iota(jnp.int32, (D, D), 1)
    ).astype(jnp.float32).astype(jnp.bfloat16)
    for tile in range(KTILES):
        kt[tile] = dot(ident, ks[tile], NT).astype(jnp.bfloat16)
    dks[...] = jnp.zeros_like(dks)
    dvs[...] = jnp.zeros_like(dvs)
    sums[...] = jnp.zeros_like(sums)
    dqt[...] = jnp.zeros_like(dqt)

    key_row = lax.broadcasted_iota(jnp.int32, (KEYS, QUERIES), 0)
    query_lane = lax.broadcasted_iota(jnp.int32, (1, QUERIES), 1)

    def scores(n, carry):
        made = []
        for step in range(UNROLL):
            i = list_ref[0, n * UNROLL + step]
            j = list_ref[1, n * UNROLL + step]
            at = i * QUERIES + query_lane
            key = key_row + j * KEYS
            seen = (key <= at) & (key >= begin(at))
            e = jnp.exp2(dot(ks[j], qs[i], NT) * (SCALE * LOG2E))
            e = jnp.concatenate(
                [jnp.where(seen, e[:, :QUERIES], 0.0), jnp.where(seen, e[:, QUERIES:], 0.0)],
                axis=1,
            )
            made.append((i, e, jnp.sum(e.reshape(KEYS // 8, 8, 2 * QUERIES), axis=0)))
        for step, (i, e, total) in enumerate(made):
            es[n * UNROLL + step] = e
            sums[i] += total
        return carry

    lax.fori_loop(0, trips, scores, 0)
    for i in range(QTILES):
        sums[i, 0:1, :] = 1.0 / jnp.sum(sums[i], axis=0, keepdims=True)

    def grads(n, carry):
        made = []
        for step in range(UNROLL):
            i = list_ref[0, n * UNROLL + step]
            j = list_ref[1, n * UNROLL + step]
            p = es[n * UNROLL + step] * sums[i, 0:1, :]
            dp = dot(vs[j], gs[i], NT)
            ds = (p * (dp - dt[i])).astype(jnp.bfloat16)
            p = p.astype(jnp.bfloat16)
            made.append((i, j, dot(p, gs[i]), dot(ds, qs[i]), dot(kt[j], ds)))
        for i, j, dv, dk, dq in made:
            dvs[j] += dv
            dks[j] += dk
            dqt[i] += dq
        return carry

    lax.fori_loop(0, trips, grads, 0)

    for i in range(QTILES):
        dqs[i] = jnp.transpose(dqt[i] * SCALE).astype(jnp.bfloat16)
    for src, places in pieces():
        mine, other = [], []
        for at in places:
            tile, off = at // KEYS, at % KEYS
            dk = dks[tile, off : off + 16, :] * SCALE
            dv = dvs[tile, off : off + 16, :]
            mine.append(jnp.where(core == 0, dk, dv).astype(jnp.bfloat16))
            other.append(jnp.where(core == 0, dv, dk).astype(jnp.bfloat16))
        both = jnp.concatenate(
            [jnp.concatenate(mine, axis=0), jnp.concatenate(other, axis=0)], axis=1
        )
        both = dot(swap, both).astype(jnp.bfloat16)
        keep_ref[src] = both[:, :D].reshape(16, 16, D)
        give_ref[src] = both[:, D:].reshape(16, 16, D)


def unsort_kernel(dqs, back_ref):
    swap = swap_matrix(4)
    for src, places in pieces():
        heads = [
            jnp.concatenate(
                [
                    dqs[at // QUERIES, at % QUERIES + h * QUERIES : at % QUERIES + h * QUERIES + 16]
                    for at in places
                ],
                axis=0,
            )
            for h in range(2)
        ]
        both = dot(swap, jnp.concatenate(heads, axis=1)).astype(jnp.bfloat16)
        back_ref[src, 0:16, :] = both[:, :D].reshape(16, 16, D)
        back_ref[src, 16:32, :] = both[:, D:].reshape(16, 16, D)


def add_kernel(back_ref, mine_ref, other_ref, out_ref):
    total = mine_ref[...].astype(jnp.float32) + other_ref[...].astype(jnp.float32)
    out_ref[...] = total.astype(jnp.bfloat16)


def unpack_kernel(slot_ref, back_ref, q_hbm, k_hbm, v_hbm, qs, ks, vs, sent):
    plan = jnp.transpose(plan_matrix(slot_ref)).astype(jnp.bfloat16)
    both = jnp.concatenate([plan, plan], axis=1)
    copies = []
    for core, out in ((0, ks), (1, vs)):
        for b in range(4):
            rows = jnp.concatenate(
                [
                    back_ref[:, core, :, b, high, 32:48, :].reshape(ROWS, D)
                    for high in range(2)
                ],
                axis=0,
            )
            out[:, b * D : (b + 1) * D] = dot(both, rows).astype(jnp.bfloat16)
        far = (k_hbm, v_hbm)[core]
        copies.append(pltpu.make_async_copy(out, far, sent.at[4 + core]))
        copies[-1].start()
    for b in range(4):
        for head in range(8):
            high, core, h = head // 4, (head // 2) % 2, head % 2
            rows = back_ref[:, core, :, b, high, h * 16 : h * 16 + 16, :].reshape(ROWS, D)
            qs[b, :, head * D : (head + 1) * D] = dot(plan, rows).astype(jnp.bfloat16)
        far = q_hbm.at[:, pl.ds(b * 8 * D, 8 * D)]
        copies.append(pltpu.make_async_copy(qs.at[b], far, sent.at[b]))
        copies[-1].start()
    for copy in copies:
        copy.wait()


def swapped(array):
    return lax.ppermute(array, "dp", [(i, i ^ 1) for i in range(8)])


def vmem(count):
    return [pl.BlockSpec(memory_space=pltpu.VMEM)] * count


SMEM = pl.BlockSpec(memory_space=pltpu.SMEM)
PARAMS = pltpu.CompilerParams(vmem_limit_bytes=VMEM)


def cost(flops, size):
    return pl.CostEstimate(flops=flops, bytes_accessed=size, transcendentals=0)


def take(recv):
    return pl.pallas_call(
        take_kernel,
        grid=(4,),
        in_specs=[pl.BlockSpec((32, 16, D), lambda i: (i, 4, 0))],
        out_specs=pl.BlockSpec((32, 16, D), lambda i: (i, 0, 0)),
        out_shape=jax.ShapeDtypeStruct((128, 16, D), jnp.bfloat16),
        compiler_params=PARAMS,
        name="take",
    )(recv)


def sort(info, recv):
    bf, f32 = jnp.bfloat16, jnp.float32
    return pl.pallas_call(
        sort_kernel,
        in_specs=[SMEM] + vmem(1),
        out_specs=vmem(3),
        out_shape=[
            jax.ShapeDtypeStruct((QTILES, 2 * QUERIES, D), bf),
            jax.ShapeDtypeStruct((QTILES, 2 * QUERIES, D), bf),
            jax.ShapeDtypeStruct((QTILES, 1, 2 * QUERIES), f32),
        ],
        scratch_shapes=[pltpu.VMEM((TOKENS, D), bf)],
        compiler_params=PARAMS,
        cost_estimate=cost(10**9, 6 * 10**6),
        name="sort",
    )(info, recv)


def attention(info, near, far, mine, other, q, g, delta):
    bf, f32 = jnp.bfloat16, jnp.float32
    pairs = sum(i * QUERIES // KEYS + 1 for i in range(QTILES)) + UNROLL
    return pl.pallas_call(
        attention_kernel,
        in_specs=[SMEM] * 3 + vmem(5),
        out_specs=vmem(3),
        out_shape=[
            jax.ShapeDtypeStruct((QTILES, 2 * QUERIES, D), bf),
            jax.ShapeDtypeStruct((128, 16, D), bf),
            jax.ShapeDtypeStruct((128, 16, D), bf),
        ],
        scratch_shapes=[
            pltpu.VMEM((KTILES, KEYS, D), bf),
            pltpu.VMEM((KTILES, KEYS, D), bf),
            pltpu.VMEM((KTILES, D, KEYS), bf),
            pltpu.VMEM((pairs, KEYS, 2 * QUERIES), f32),
            pltpu.VMEM((KTILES, KEYS, D), f32),
            pltpu.VMEM((KTILES, KEYS, D), f32),
            pltpu.VMEM((QTILES, D, 2 * QUERIES), f32),
            pltpu.VMEM((QTILES, 8, 2 * QUERIES), f32),
            pltpu.SMEM((2, pairs), jnp.int32),
        ],
        compiler_params=PARAMS,
        cost_estimate=cost(4 * 10**9, 10**7),
        name="attention",
    )(info, near, far, mine, other, q, g, delta)


def unsort(dq):
    return pl.pallas_call(
        unsort_kernel,
        in_specs=vmem(1),
        out_specs=vmem(1)[0],
        out_shape=jax.ShapeDtypeStruct((128, 48, D), jnp.bfloat16),
        compiler_params=PARAMS,
        cost_estimate=cost(10**9, 4 * 10**6),
        name="unsort",
    )(dq)


def add(back, mine, other):
    part = pl.BlockSpec((32, 16, D), lambda i: (i, 0, 0))
    return pl.pallas_call(
        add_kernel,
        grid=(4,),
        in_specs=[pl.BlockSpec(memory_space=pl.ANY), part, part],
        out_specs=pl.BlockSpec((32, 16, D), lambda i: (i, 2, 0)),
        out_shape=jax.ShapeDtypeStruct((128, 48, D), jnp.bfloat16),
        input_output_aliases={0: 0},
        compiler_params=PARAMS,
        name="add",
    )(back, mine, other)


HBM = pl.BlockSpec(memory_space=pltpu.HBM)


def pack(slot, q, o, g, k, v):
    bf = jnp.bfloat16
    return pl.pallas_call(
        pack_kernel,
        in_specs=vmem(1) + [HBM] * 5,
        out_specs=vmem(1)[0],
        out_shape=jax.ShapeDtypeStruct((*CUT, 88, D), bf),
        scratch_shapes=[pltpu.VMEM((4, ROWS, 8 * D), bf)] * 3
        + [pltpu.VMEM((ROWS, 4 * D), bf)] * 2
        + [pltpu.SemaphoreType.DMA((14,))],
        compiler_params=pltpu.CompilerParams(vmem_limit_bytes=60 * 1024 * 1024),
        name="pack",
    )(slot, q, o, g, k, v)


def unpack(slot, back):
    bf = jnp.bfloat16
    return pl.pallas_call(
        unpack_kernel,
        in_specs=vmem(2),
        out_specs=[HBM] * 3,
        out_shape=[
            jax.ShapeDtypeStruct((ROWS, 32 * D), bf),
            jax.ShapeDtypeStruct((ROWS, 4 * D), bf),
            jax.ShapeDtypeStruct((ROWS, 4 * D), bf),
        ],
        scratch_shapes=[
            pltpu.VMEM((4, ROWS, 8 * D), bf),
            pltpu.VMEM((ROWS, 4 * D), bf),
            pltpu.VMEM((ROWS, 4 * D), bf),
            pltpu.SemaphoreType.DMA((6,)),
        ],
        compiler_params=PARAMS,
        name="unpack",
    )(slot, back)


def per_device(queries, keys, values, attn_out, out_grad, send_slot, proof_length_list):
    core = lax.axis_index("dp") & 1
    ctx = lax.axis_index("ctx")
    info = jnp.stack([core, (ctx & 1) * 2 + core, ctx >> 3 == core]).astype(jnp.int32)
    lengths = swapped(proof_length_list)

    send = pack(send_slot, queries, attn_out, out_grad, keys, values)
    recv = lax.all_to_all(
        send.reshape(128, 88, D), ("dp", "ctx"), split_axis=0, concat_axis=0, tiled=True
    )
    mine = take(recv)
    other = swapped(mine)
    q, g, delta = sort(info, recv)
    dq, keep, give = attention(info, proof_length_list, lengths, mine, other, q, g, delta)
    back = add(unsort(dq), keep, swapped(give))
    back = lax.all_to_all(back, ("dp", "ctx"), split_axis=0, concat_axis=0, tiled=True)
    return unpack(send_slot, back.reshape(*CUT, 48, D))


def solution(mesh):
    rows = P(("dp", "ctx"), None)
    return jax.shard_map(
        per_device,
        mesh=mesh,
        in_specs=(rows, rows, rows, rows, rows, rows, P("dp", None)),
        out_specs=(rows, rows, rows),
        check_vma=False,
    )
```

```python
import jax
import jax.numpy as jnp
from jax import lax
from jax.experimental import pallas as pl
from jax.experimental.pallas import tpu as pltpu
from jax.sharding import PartitionSpec as P

D = 128
ROWS = 128
KEYS = 256
QUERIES = 256
TOKENS = 2048
KTILES = TOKENS // KEYS
QTILES = TOKENS // QUERIES
UNROLL = 11
TAIL = 4
AHEAD = 1
CUT = (4, 2, 2, 4, 2)
SCALE = D ** (-0.5)
LOG2E = 1.4426950408889634
VMEM = 32 * 1024 * 1024
NT = (((1,), (1,)), ((), ()))
NN = (((1,), (0,)), ((), ()))


def dot(a, b, dims=NN):
    return lax.dot_general(a, b, dims, preferred_element_type=jnp.float32)


def plan_matrix(slot_ref):
    p = lax.broadcasted_iota(jnp.int32, (ROWS, ROWS), 0)
    return (p == slot_ref[...]).astype(jnp.float32)


def pack_kernel(
    slot_ref, q_hbm, o_hbm, g_hbm, k_hbm, v_hbm, out_ref, qs, os, gs, ks, vs, arrived
):
    copies = []
    for b in range(4):
        cols = pl.ds(b * 8 * D, 8 * D)
        for n, (far, near) in enumerate(((q_hbm, qs), (g_hbm, gs), (o_hbm, os))):
            copies.append(
                pltpu.make_async_copy(far.at[:, cols], near.at[b], arrived.at[b * 3 + n])
            )
    copies.append(pltpu.make_async_copy(k_hbm, ks, arrived.at[12]))
    copies.append(pltpu.make_async_copy(v_hbm, vs, arrived.at[13]))
    for copy in copies:
        copy.start()
    plan = plan_matrix(slot_ref).astype(jnp.bfloat16)
    lane = lax.broadcasted_iota(jnp.int32, (ROWS, D), 1)

    def placed(columns):
        return dot(plan, columns).astype(jnp.bfloat16).reshape(4, 2, 16, D)

    for b in range(4):
        for copy in copies[b * 3 : b * 3 + 3]:
            copy.wait()
        delta = jnp.zeros((ROWS, D), jnp.float32)
        for head in range(8):
            high, core, h = head // 4, (head // 2) % 2, head % 2
            cols = slice(head * D, (head + 1) * D)
            g = gs[b, :, cols]
            out_ref[:, core, :, b, high, h * 16 : h * 16 + 16, :] = placed(qs[b, :, cols])
            out_ref[:, core, :, b, high, 32 + h * 16 : 48 + h * 16, :] = placed(g)
            total = jnp.sum(
                os[b, :, cols].astype(jnp.float32) * g.astype(jnp.float32), axis=1, keepdims=True
            )
            delta = jnp.where(lane == head, total, delta)
        first = delta.astype(jnp.bfloat16).astype(jnp.float32)
        second = (delta - first).astype(jnp.bfloat16).astype(jnp.float32)
        third = delta - first - second
        parts = first + pltpu.roll(second, 8, 1) + pltpu.roll(third, 16, 1)
        parts = dot(plan, parts.astype(jnp.bfloat16)).reshape(8, 16, D)
        parts = (parts[:, :8] + pltpu.roll(parts[:, 8:], 64, 2)).astype(jnp.bfloat16)
        parts = parts.reshape(4, 2, 8, D)
        for high in range(2):
            for core in range(2):
                out_ref[:, core, :, b, high, 80:88, :] = parts
    copies[12].wait()
    copies[13].wait()
    for b in range(4):
        cols = slice(b * D, (b + 1) * D)
        for core, rows in ((0, ks), (1, vs)):
            rows = placed(rows[:, cols])
            for high in range(2):
                out_ref[:, core, :, b, high, 64:80, :] = rows


def swap_matrix(bits):
    size = 16 << bits
    r = lax.broadcasted_iota(jnp.int32, (size, size), 0)
    c = lax.broadcasted_iota(jnp.int32, (size, size), 1)
    same = ((r >> 4) == (c & ((1 << bits) - 1))) & ((r & 15) == (c >> bits))
    return same.astype(jnp.float32).astype(jnp.bfloat16)


def pieces():
    for half in range(2):
        for part in range(4):
            first = half * 64 + part * 16
            yield (
                slice(first, first + 16),
                [(c if half == 0 else 31 - c) * 64 + part * 16 for c in range(16)],
            )


def take_kernel(recv_ref, out_ref):
    out_ref[...] = recv_ref[...]


def sort_kernel(info_ref, recv_ref, qs, gs, dt, ds):
    swap = swap_matrix(4)
    short = swap_matrix(3)
    for src, places in pieces():

        def rows(n):
            return recv_ref[src, n * 16 : n * 16 + 16, :].reshape(256, D)

        for n, out in ((0, qs), (2, gs)):
            both = jnp.concatenate([rows(n), rows(n + 1)], axis=1)
            both = dot(swap, both).astype(jnp.bfloat16)
            for c, at in enumerate(places):
                tile, off = at // QUERIES, at % QUERIES
                r = slice(c * 16, c * 16 + 16)
                out[tile, off : off + 16, :] = both[r, :D]
                out[tile, QUERIES + off : QUERIES + off + 16, :] = both[r, D:]
        d = recv_ref[src, 80:88, :].reshape(128, D)
        d = dot(short, d).astype(jnp.bfloat16)
        for c, at in enumerate(places):
            ds[at : at + 16, :] = d[(c % 8) * 16 : (c % 8) * 16 + 16]
    row = lax.broadcasted_iota(jnp.int32, (16, D), 0)
    lane = lax.broadcasted_iota(jnp.int32, (16, D), 1)
    pick = ((lane & 7) == info_ref[1] * 2 + row) & ((lane & 63) < 24) & (row < 2)
    for tile in range(QTILES):
        at = tile * QUERIES
        upper = int(512 <= at < 1536)
        own = (pick & (lane >> 6 == upper)).astype(jnp.float32).astype(jnp.bfloat16)
        d = dot(own, ds[at : at + QUERIES, :], NT)
        dt[tile] = jnp.concatenate([d[0:1], d[1:2]], axis=1)


def attention_kernel(
    info_ref, near_ref, far_ref, mine_ref, other_ref, qs, gs, dt, dqs, keep_ref, give_ref,
    ks, vs, kt, es, dks, dvs, dqt, sums, list_ref,
):
    core = info_ref[0]
    lengths = [jnp.where(info_ref[2] == 1, near_ref[0, n], far_ref[0, n]) for n in range(3)]
    end0 = lengths[0]
    end1 = end0 + lengths[1]
    end2 = end1 + lengths[2]

    def begin(at):
        return jnp.where(
            at >= end2, end2, jnp.where(at >= end1, end1, jnp.where(at >= end0, end0, 0))
        )

    count = jnp.int32(0)
    for i in range(QTILES):
        last = i * QUERIES // KEYS
        first = begin(jnp.int32(i * QUERIES)) // KEYS
        for j in range(last + 1):
            list_ref[0, count] = i
            list_ref[1, count] = j
            count = count + (j >= first).astype(jnp.int32)
    for extra in range(UNROLL + TAIL):
        list_ref[0, count + extra] = 0
        list_ref[1, count + extra] = KTILES - 1
    trips = (count + UNROLL // 2) // UNROLL
    rest = (jnp.maximum(count - trips * UNROLL, 0) + TAIL - 1) // TAIL

    def for_pairs(body):
        lax.fori_loop(0, trips, lambda n, c: body(n * UNROLL, UNROLL) or c, 0)
        lax.fori_loop(0, rest, lambda n, c: body(trips * UNROLL + n * TAIL, TAIL) or c, 0)

    swap = swap_matrix(4)
    for src, places in pieces():
        mine = mine_ref[src].reshape(256, D)
        other = other_ref[src].reshape(256, D)
        both = jnp.concatenate(
            [jnp.where(core == 0, mine, other), jnp.where(core == 0, other, mine)], axis=1
        )
        both = dot(swap, both).astype(jnp.bfloat16)
        for c, at in enumerate(places):
            tile, off = at // KEYS, at % KEYS
            ks[tile, off : off + 16, :] = both[c * 16 : c * 16 + 16, :D]
            vs[tile, off : off + 16, :] = both[c * 16 : c * 16 + 16, D:]
    ident = (
        lax.broadcasted_iota(jnp.int32, (D, D), 0) == lax.broadcasted_iota(jnp.int32, (D, D), 1)
    ).astype(jnp.float32).astype(jnp.bfloat16)
    for tile in range(KTILES):
        kt[tile] = dot(ident, ks[tile], NT).astype(jnp.bfloat16)
    dks[...] = jnp.zeros_like(dks)
    dvs[...] = jnp.zeros_like(dvs)
    sums[...] = jnp.zeros_like(sums)
    dqt[...] = jnp.zeros_like(dqt)

    key_row = lax.broadcasted_iota(jnp.int32, (KEYS, QUERIES), 0)
    query_lane = lax.broadcasted_iota(jnp.int32, (1, QUERIES), 1)

    def pair(n):
        return list_ref[0, n], list_ref[1, n]

    def ahead(count, start):
        begun = [start(step) for step in range(min(AHEAD, count))]
        for step in range(count):
            if step + AHEAD < count:
                begun.append(start(step + AHEAD))
            yield step, begun[step]

    def scores(first, number):
        pairs = [pair(first + step) for step in range(number)]
        made = []
        for step, s in ahead(number, lambda step: dot(ks[pairs[step][1]], qs[pairs[step][0]], NT)):
            i, j = pairs[step]
            at = i * QUERIES + query_lane
            key = key_row + j * KEYS
            seen = (key <= at) & (key >= begin(at))
            e = jnp.exp2(s * (SCALE * LOG2E))
            e = jnp.concatenate(
                [jnp.where(seen, e[:, :QUERIES], 0.0), jnp.where(seen, e[:, QUERIES:], 0.0)],
                axis=1,
            )
            es[first + step] = e
            made.append((i, jnp.sum(e.reshape(KEYS // 8, 8, 2 * QUERIES), axis=0)))
        for i, total in made:
            sums[i] += total

    for_pairs(scores)
    for i in range(QTILES):
        sums[i, 0:1, :] = 1.0 / jnp.sum(sums[i], axis=0, keepdims=True)

    def grads(first, number):
        pairs = [pair(first + step) for step in range(number)]
        made = []
        for step, dp in ahead(number, lambda step: dot(vs[pairs[step][1]], gs[pairs[step][0]], NT)):
            i, j = pairs[step]
            p = es[first + step] * sums[i, 0:1, :]
            ds = (p * (dp - dt[i])).astype(jnp.bfloat16)
            p = p.astype(jnp.bfloat16)
            made.append((i, j, dot(p, gs[i]), dot(ds, qs[i]), dot(kt[j], ds)))
        for i, j, dv, dk, dq in made:
            dvs[j] += dv
            dks[j] += dk
            dqt[i] += dq

    for_pairs(grads)
    for i in range(QTILES):
        dqs[i] = jnp.transpose(dqt[i] * SCALE).astype(jnp.bfloat16)
    for src, places in pieces():
        mine, other = [], []
        for at in places:
            tile, off = at // KEYS, at % KEYS
            dk = dks[tile, off : off + 16, :] * SCALE
            dv = dvs[tile, off : off + 16, :]
            mine.append(jnp.where(core == 0, dk, dv).astype(jnp.bfloat16))
            other.append(jnp.where(core == 0, dv, dk).astype(jnp.bfloat16))
        both = jnp.concatenate(
            [jnp.concatenate(mine, axis=0), jnp.concatenate(other, axis=0)], axis=1
        )
        both = dot(swap, both).astype(jnp.bfloat16)
        keep_ref[src] = both[:, :D].reshape(16, 16, D)
        give_ref[src] = both[:, D:].reshape(16, 16, D)


def unsort_kernel(dqs, back_ref):
    swap = swap_matrix(4)
    for src, places in pieces():
        heads = [
            jnp.concatenate(
                [
                    dqs[at // QUERIES, at % QUERIES + h * QUERIES : at % QUERIES + h * QUERIES + 16]
                    for at in places
                ],
                axis=0,
            )
            for h in range(2)
        ]
        both = dot(swap, jnp.concatenate(heads, axis=1)).astype(jnp.bfloat16)
        back_ref[src, 0:16, :] = both[:, :D].reshape(16, 16, D)
        back_ref[src, 16:32, :] = both[:, D:].reshape(16, 16, D)


def add_kernel(back_ref, mine_ref, other_ref, out_ref):
    total = mine_ref[...].astype(jnp.float32) + other_ref[...].astype(jnp.float32)
    out_ref[...] = total.astype(jnp.bfloat16)


def unpack_kernel(slot_ref, back_ref, q_hbm, k_hbm, v_hbm, qs, ks, vs, sent):
    plan = jnp.transpose(plan_matrix(slot_ref)).astype(jnp.bfloat16)
    both = jnp.concatenate([plan, plan], axis=1)
    copies = []
    for core, out in ((0, ks), (1, vs)):
        for b in range(4):
            rows = jnp.concatenate(
                [
                    back_ref[:, core, :, b, high, 32:48, :].reshape(ROWS, D)
                    for high in range(2)
                ],
                axis=0,
            )
            out[:, b * D : (b + 1) * D] = dot(both, rows).astype(jnp.bfloat16)
        far = (k_hbm, v_hbm)[core]
        copies.append(pltpu.make_async_copy(out, far, sent.at[4 + core]))
        copies[-1].start()
    for b in range(4):
        for head in range(8):
            high, core, h = head // 4, (head // 2) % 2, head % 2
            rows = back_ref[:, core, :, b, high, h * 16 : h * 16 + 16, :].reshape(ROWS, D)
            qs[b, :, head * D : (head + 1) * D] = dot(plan, rows).astype(jnp.bfloat16)
        far = q_hbm.at[:, pl.ds(b * 8 * D, 8 * D)]
        copies.append(pltpu.make_async_copy(qs.at[b], far, sent.at[b]))
        copies[-1].start()
    for copy in copies:
        copy.wait()


def swapped(array):
    return lax.ppermute(array, "dp", [(i, i ^ 1) for i in range(8)])


def vmem(count):
    return [pl.BlockSpec(memory_space=pltpu.VMEM)] * count


SMEM = pl.BlockSpec(memory_space=pltpu.SMEM)
PARAMS = pltpu.CompilerParams(vmem_limit_bytes=VMEM)
WIDE = pltpu.CompilerParams(vmem_limit_bytes=42 * 1024 * 1024)


def cost(flops, size):
    return pl.CostEstimate(flops=flops, bytes_accessed=size, transcendentals=0)


def take(recv):
    return pl.pallas_call(
        take_kernel,
        grid=(4,),
        in_specs=[pl.BlockSpec((32, 16, D), lambda i: (i, 4, 0))],
        out_specs=pl.BlockSpec((32, 16, D), lambda i: (i, 0, 0)),
        out_shape=jax.ShapeDtypeStruct((128, 16, D), jnp.bfloat16),
        compiler_params=PARAMS,
        name="take",
    )(recv)


def sort(info, recv):
    bf, f32 = jnp.bfloat16, jnp.float32
    return pl.pallas_call(
        sort_kernel,
        in_specs=[SMEM] + vmem(1),
        out_specs=vmem(3),
        out_shape=[
            jax.ShapeDtypeStruct((QTILES, 2 * QUERIES, D), bf),
            jax.ShapeDtypeStruct((QTILES, 2 * QUERIES, D), bf),
            jax.ShapeDtypeStruct((QTILES, 1, 2 * QUERIES), f32),
        ],
        scratch_shapes=[pltpu.VMEM((TOKENS, D), bf)],
        compiler_params=PARAMS,
        cost_estimate=cost(10**9, 6 * 10**6),
        name="sort",
    )(info, recv)


def attention(info, near, far, mine, other, q, g, delta):
    bf, f32 = jnp.bfloat16, jnp.float32
    pairs = sum(i * QUERIES // KEYS + 1 for i in range(QTILES)) + UNROLL + TAIL
    return pl.pallas_call(
        attention_kernel,
        in_specs=[SMEM] * 3 + vmem(5),
        out_specs=vmem(3),
        out_shape=[
            jax.ShapeDtypeStruct((QTILES, 2 * QUERIES, D), bf),
            jax.ShapeDtypeStruct((128, 16, D), bf),
            jax.ShapeDtypeStruct((128, 16, D), bf),
        ],
        scratch_shapes=[
            pltpu.VMEM((KTILES, KEYS, D), bf),
            pltpu.VMEM((KTILES, KEYS, D), bf),
            pltpu.VMEM((KTILES, D, KEYS), bf),
            pltpu.VMEM((pairs, KEYS, 2 * QUERIES), f32),
            pltpu.VMEM((KTILES, KEYS, D), f32),
            pltpu.VMEM((KTILES, KEYS, D), f32),
            pltpu.VMEM((QTILES, D, 2 * QUERIES), f32),
            pltpu.VMEM((QTILES, 8, 2 * QUERIES), f32),
            pltpu.SMEM((2, pairs), jnp.int32),
        ],
        compiler_params=WIDE,
        cost_estimate=cost(4 * 10**9, 10**7),
        name="attention",
    )(info, near, far, mine, other, q, g, delta)


def unsort(dq):
    return pl.pallas_call(
        unsort_kernel,
        in_specs=vmem(1),
        out_specs=vmem(1)[0],
        out_shape=jax.ShapeDtypeStruct((128, 48, D), jnp.bfloat16),
        compiler_params=PARAMS,
        cost_estimate=cost(10**9, 4 * 10**6),
        name="unsort",
    )(dq)


def add(back, mine, other):
    part = pl.BlockSpec((32, 16, D), lambda i: (i, 0, 0))
    return pl.pallas_call(
        add_kernel,
        grid=(4,),
        in_specs=[pl.BlockSpec(memory_space=pl.ANY), part, part],
        out_specs=pl.BlockSpec((32, 16, D), lambda i: (i, 2, 0)),
        out_shape=jax.ShapeDtypeStruct((128, 48, D), jnp.bfloat16),
        input_output_aliases={0: 0},
        compiler_params=PARAMS,
        name="add",
    )(back, mine, other)


HBM = pl.BlockSpec(memory_space=pltpu.HBM)


def pack(slot, q, o, g, k, v):
    bf = jnp.bfloat16
    return pl.pallas_call(
        pack_kernel,
        in_specs=vmem(1) + [HBM] * 5,
        out_specs=vmem(1)[0],
        out_shape=pltpu.VMEM((*CUT, 88, D), bf),
        scratch_shapes=[pltpu.VMEM((4, ROWS, 8 * D), bf)] * 3
        + [pltpu.VMEM((ROWS, 4 * D), bf)] * 2
        + [pltpu.SemaphoreType.DMA((14,))],
        compiler_params=pltpu.CompilerParams(vmem_limit_bytes=60 * 1024 * 1024),
        name="pack",
    )(slot, q, o, g, k, v)


def unpack(slot, back):
    bf = jnp.bfloat16
    return pl.pallas_call(
        unpack_kernel,
        in_specs=vmem(2),
        out_specs=[HBM] * 3,
        out_shape=[
            jax.ShapeDtypeStruct((ROWS, 32 * D), bf),
            jax.ShapeDtypeStruct((ROWS, 4 * D), bf),
            jax.ShapeDtypeStruct((ROWS, 4 * D), bf),
        ],
        scratch_shapes=[
            pltpu.VMEM((4, ROWS, 8 * D), bf),
            pltpu.VMEM((ROWS, 4 * D), bf),
            pltpu.VMEM((ROWS, 4 * D), bf),
            pltpu.SemaphoreType.DMA((6,)),
        ],
        compiler_params=PARAMS,
        name="unpack",
    )(slot, back)


def per_device(queries, keys, values, attn_out, out_grad, send_slot, proof_length_list):
    core = lax.axis_index("dp") & 1
    ctx = lax.axis_index("ctx")
    info = jnp.stack([core, (ctx & 1) * 2 + core, ctx >> 3 == core]).astype(jnp.int32)
    lengths = swapped(proof_length_list)

    send = pack(send_slot, queries, attn_out, out_grad, keys, values)
    recv = lax.all_to_all(
        send.reshape(128, 88, D), ("dp", "ctx"), split_axis=0, concat_axis=0, tiled=True
    )
    mine = take(recv)
    other = swapped(mine)
    q, g, delta = sort(info, recv)
    dq, keep, give = attention(info, proof_length_list, lengths, mine, other, q, g, delta)
    back = add(unsort(dq), keep, swapped(give))
    back = lax.all_to_all(back, ("dp", "ctx"), split_axis=0, concat_axis=0, tiled=True)
    return unpack(send_slot, back.reshape(*CUT, 48, D))


def solution(mesh):
    rows = P(("dp", "ctx"), None)
    return jax.shard_map(
        per_device,
        mesh=mesh,
        in_specs=(rows, rows, rows, rows, rows, rows, P("dp", None)),
        out_specs=(rows, rows, rows),
        check_vma=False,
    )
```

```python
import jax
import jax.numpy as jnp
from jax import lax
from jax.experimental import pallas as pl
from jax.experimental.pallas import tpu as pltpu
from jax.sharding import PartitionSpec as P

D = 128
ROWS = 128
KEYS = 256
QUERIES = 256
TOKENS = 2048
KTILES = TOKENS // KEYS
QTILES = TOKENS // QUERIES
UNROLL = 11
TAIL = 4
AHEAD = 1
CUT = (4, 2, 2, 4, 2)
SCALE = D ** (-0.5)
LOG2E = 1.4426950408889634
VMEM = 32 * 1024 * 1024
NT = (((1,), (1,)), ((), ()))
NN = (((1,), (0,)), ((), ()))


def dot(a, b, dims=NN):
    return lax.dot_general(a, b, dims, preferred_element_type=jnp.float32)


def plan_matrix(slot_ref):
    p = lax.broadcasted_iota(jnp.int32, (ROWS, ROWS), 0)
    return (p == slot_ref[...]).astype(jnp.float32)


def pack_kernel(
    slot_hbm, q_hbm, o_hbm, g_hbm, k_hbm, v_hbm, out_ref, slot, qs, os, gs, ks, vs, arrived
):
    copies = []
    for b in range(4):
        cols = pl.ds(b * 8 * D, 8 * D)
        for n, (far, near) in enumerate(((q_hbm, qs), (g_hbm, gs), (o_hbm, os))):
            copies.append(
                pltpu.make_async_copy(far.at[:, cols], near.at[b], arrived.at[b * 3 + n])
            )
    copies.append(pltpu.make_async_copy(k_hbm, ks, arrived.at[12]))
    copies.append(pltpu.make_async_copy(v_hbm, vs, arrived.at[13]))
    first = pltpu.make_async_copy(slot_hbm, slot, arrived.at[14])
    first.start()
    for copy in copies:
        copy.start()
    first.wait()
    plan = plan_matrix(slot).astype(jnp.bfloat16)
    lane = lax.broadcasted_iota(jnp.int32, (ROWS, D), 1)

    def placed(columns):
        return dot(plan, columns).astype(jnp.bfloat16).reshape(4, 2, 16, D)

    for b in range(4):
        for copy in copies[b * 3 : b * 3 + 3]:
            copy.wait()
        delta = jnp.zeros((ROWS, D), jnp.float32)
        for head in range(8):
            high, core, h = head // 4, (head // 2) % 2, head % 2
            cols = slice(head * D, (head + 1) * D)
            g = gs[b, :, cols]
            out_ref[:, core, :, b, high, h * 16 : h * 16 + 16, :] = placed(qs[b, :, cols])
            out_ref[:, core, :, b, high, 32 + h * 16 : 48 + h * 16, :] = placed(g)
            total = jnp.sum(
                os[b, :, cols].astype(jnp.float32) * g.astype(jnp.float32), axis=1, keepdims=True
            )
            delta = jnp.where(lane == head, total, delta)
        first = delta.astype(jnp.bfloat16).astype(jnp.float32)
        second = (delta - first).astype(jnp.bfloat16).astype(jnp.float32)
        third = delta - first - second
        parts = first + pltpu.roll(second, 8, 1) + pltpu.roll(third, 16, 1)
        parts = dot(plan, parts.astype(jnp.bfloat16)).reshape(8, 16, D)
        parts = (parts[:, :8] + pltpu.roll(parts[:, 8:], 64, 2)).astype(jnp.bfloat16)
        parts = parts.reshape(4, 2, 8, D)
        for high in range(2):
            for core in range(2):
                out_ref[:, core, :, b, high, 80:88, :] = parts
    copies[12].wait()
    copies[13].wait()
    for b in range(4):
        cols = slice(b * D, (b + 1) * D)
        for core, rows in ((0, ks), (1, vs)):
            rows = placed(rows[:, cols])
            for high in range(2):
                out_ref[:, core, :, b, high, 64:80, :] = rows


def swap_matrix(bits):
    size = 16 << bits
    r = lax.broadcasted_iota(jnp.int32, (size, size), 0)
    c = lax.broadcasted_iota(jnp.int32, (size, size), 1)
    same = ((r >> 4) == (c & ((1 << bits) - 1))) & ((r & 15) == (c >> bits))
    return same.astype(jnp.float32).astype(jnp.bfloat16)


def pieces():
    for half in range(2):
        for part in range(4):
            first = half * 64 + part * 16
            yield (
                slice(first, first + 16),
                [(c if half == 0 else 31 - c) * 64 + part * 16 for c in range(16)],
            )


def take_kernel(recv_ref, out_ref):
    out_ref[...] = recv_ref[...]


def sort_kernel(info_ref, recv_ref, qs, gs, dt, ds):
    swap = swap_matrix(4)
    short = swap_matrix(3)
    for src, places in pieces():

        def rows(n):
            return recv_ref[src, n * 16 : n * 16 + 16, :].reshape(256, D)

        for n, out in ((0, qs), (2, gs)):
            both = jnp.concatenate([rows(n), rows(n + 1)], axis=1)
            both = dot(swap, both).astype(jnp.bfloat16)
            for c, at in enumerate(places):
                tile, off = at // QUERIES, at % QUERIES
                r = slice(c * 16, c * 16 + 16)
                out[tile, off : off + 16, :] = both[r, :D]
                out[tile, QUERIES + off : QUERIES + off + 16, :] = both[r, D:]
        d = recv_ref[src, 80:88, :].reshape(128, D)
        d = dot(short, d).astype(jnp.bfloat16)
        for c, at in enumerate(places):
            ds[at : at + 16, :] = d[(c % 8) * 16 : (c % 8) * 16 + 16]
    row = lax.broadcasted_iota(jnp.int32, (16, D), 0)
    lane = lax.broadcasted_iota(jnp.int32, (16, D), 1)
    pick = ((lane & 7) == info_ref[1] * 2 + row) & ((lane & 63) < 24) & (row < 2)
    for tile in range(QTILES):
        at = tile * QUERIES
        upper = int(512 <= at < 1536)
        own = (pick & (lane >> 6 == upper)).astype(jnp.float32).astype(jnp.bfloat16)
        d = dot(own, ds[at : at + QUERIES, :], NT)
        dt[tile] = jnp.concatenate([d[0:1], d[1:2]], axis=1)


def attention_kernel(
    info_ref, near_ref, far_ref, mine_ref, other_ref, qs, gs, dt, dqt, keep_ref, give_ref,
    ks, vs, kt, es, dks, dvs, sums, list_ref,
):
    core = info_ref[0]
    lengths = [jnp.where(info_ref[2] == 1, near_ref[0, n], far_ref[0, n]) for n in range(3)]
    end0 = lengths[0]
    end1 = end0 + lengths[1]
    end2 = end1 + lengths[2]

    def begin(at):
        return jnp.where(
            at >= end2, end2, jnp.where(at >= end1, end1, jnp.where(at >= end0, end0, 0))
        )

    count = jnp.int32(0)
    for i in range(QTILES):
        last = i * QUERIES // KEYS
        first = begin(jnp.int32(i * QUERIES)) // KEYS
        for j in range(last + 1):
            list_ref[0, count] = i
            list_ref[1, count] = j
            count = count + (j >= first).astype(jnp.int32)
    for extra in range(UNROLL + TAIL):
        list_ref[0, count + extra] = 0
        list_ref[1, count + extra] = KTILES - 1
    trips = (count + UNROLL // 2) // UNROLL
    rest = (jnp.maximum(count - trips * UNROLL, 0) + TAIL - 1) // TAIL

    def for_pairs(body):
        lax.fori_loop(0, trips, lambda n, c: body(n * UNROLL, UNROLL) or c, 0)
        lax.fori_loop(0, rest, lambda n, c: body(trips * UNROLL + n * TAIL, TAIL) or c, 0)

    swap = swap_matrix(4)
    for src, places in pieces():
        mine = mine_ref[src].reshape(256, D)
        other = other_ref[src].reshape(256, D)
        both = jnp.concatenate(
            [jnp.where(core == 0, mine, other), jnp.where(core == 0, other, mine)], axis=1
        )
        both = dot(swap, both).astype(jnp.bfloat16)
        for c, at in enumerate(places):
            tile, off = at // KEYS, at % KEYS
            ks[tile, off : off + 16, :] = both[c * 16 : c * 16 + 16, :D]
            vs[tile, off : off + 16, :] = both[c * 16 : c * 16 + 16, D:]
    ident = (
        lax.broadcasted_iota(jnp.int32, (D, D), 0) == lax.broadcasted_iota(jnp.int32, (D, D), 1)
    ).astype(jnp.float32).astype(jnp.bfloat16)
    for tile in range(KTILES):
        kt[tile] = dot(ident, ks[tile], NT).astype(jnp.bfloat16)
    dks[...] = jnp.zeros_like(dks)
    dvs[...] = jnp.zeros_like(dvs)
    sums[...] = jnp.zeros_like(sums)
    dqt[...] = jnp.zeros_like(dqt)

    key_row = lax.broadcasted_iota(jnp.int32, (KEYS, QUERIES), 0)
    query_lane = lax.broadcasted_iota(jnp.int32, (1, QUERIES), 1)

    def pair(n):
        return list_ref[0, n], list_ref[1, n]

    def ahead(count, start):
        begun = [start(step) for step in range(min(AHEAD, count))]
        for step in range(count):
            if step + AHEAD < count:
                begun.append(start(step + AHEAD))
            yield step, begun[step]

    def scores(first, number):
        pairs = [pair(first + step) for step in range(number)]
        made = []
        for step, s in ahead(number, lambda step: dot(ks[pairs[step][1]], qs[pairs[step][0]], NT)):
            i, j = pairs[step]
            at = i * QUERIES + query_lane
            key = key_row + j * KEYS
            seen = (key <= at) & (key >= begin(at))
            e = jnp.exp2(s * (SCALE * LOG2E))
            e = jnp.concatenate(
                [jnp.where(seen, e[:, :QUERIES], 0.0), jnp.where(seen, e[:, QUERIES:], 0.0)],
                axis=1,
            )
            es[first + step] = e
            made.append((i, jnp.sum(e.reshape(KEYS // 8, 8, 2 * QUERIES), axis=0)))
        for i, total in made:
            sums[i] += total

    for_pairs(scores)
    for i in range(QTILES):
        sums[i, 0:1, :] = 1.0 / jnp.sum(sums[i], axis=0, keepdims=True)

    def grads(first, number):
        pairs = [pair(first + step) for step in range(number)]
        made = []
        for step, dp in ahead(number, lambda step: dot(vs[pairs[step][1]], gs[pairs[step][0]], NT)):
            i, j = pairs[step]
            p = es[first + step] * sums[i, 0:1, :]
            ds = (p * (dp - dt[i])).astype(jnp.bfloat16)
            p = p.astype(jnp.bfloat16)
            made.append((i, j, dot(p, gs[i]), dot(ds, qs[i]), dot(kt[j], ds)))
        for i, j, dv, dk, dq in made:
            dvs[j] += dv
            dks[j] += dk
            dqt[i] += dq

    for_pairs(grads)
    for src, places in pieces():
        mine, other = [], []
        for at in places:
            tile, off = at // KEYS, at % KEYS
            dk = dks[tile, off : off + 16, :] * SCALE
            dv = dvs[tile, off : off + 16, :]
            mine.append(jnp.where(core == 0, dk, dv).astype(jnp.bfloat16))
            other.append(jnp.where(core == 0, dv, dk).astype(jnp.bfloat16))
        both = jnp.concatenate(
            [jnp.concatenate(mine, axis=0), jnp.concatenate(other, axis=0)], axis=1
        )
        both = dot(swap, both).astype(jnp.bfloat16)
        keep_ref[src] = both[:, :D].reshape(16, 16, D)
        give_ref[src] = both[:, D:].reshape(16, 16, D)


def unsort_kernel(dqt, back_ref, dqs):
    for i in range(QTILES):
        dqs[i] = jnp.transpose(dqt[i] * SCALE).astype(jnp.bfloat16)
    swap = swap_matrix(4)
    for src, places in pieces():
        heads = [
            jnp.concatenate(
                [
                    dqs[at // QUERIES, at % QUERIES + h * QUERIES : at % QUERIES + h * QUERIES + 16]
                    for at in places
                ],
                axis=0,
            )
            for h in range(2)
        ]
        both = dot(swap, jnp.concatenate(heads, axis=1)).astype(jnp.bfloat16)
        back_ref[src, 0:16, :] = both[:, :D].reshape(16, 16, D)
        back_ref[src, 16:32, :] = both[:, D:].reshape(16, 16, D)


def add_kernel(back_ref, mine_ref, other_ref, out_ref):
    total = mine_ref[...].astype(jnp.float32) + other_ref[...].astype(jnp.float32)
    out_ref[...] = total.astype(jnp.bfloat16)


def unpack_kernel(slot_ref, back_ref, q_hbm, k_hbm, v_hbm, qs, ks, vs, sent):
    plan = jnp.transpose(plan_matrix(slot_ref)).astype(jnp.bfloat16)
    both = jnp.concatenate([plan, plan], axis=1)
    copies = []
    for core, out in ((0, ks), (1, vs)):
        for b in range(4):
            rows = jnp.concatenate(
                [
                    back_ref[:, core, :, b, high, 32:48, :].reshape(ROWS, D)
                    for high in range(2)
                ],
                axis=0,
            )
            out[:, b * D : (b + 1) * D] = dot(both, rows).astype(jnp.bfloat16)
        far = (k_hbm, v_hbm)[core]
        copies.append(pltpu.make_async_copy(out, far, sent.at[4 + core]))
        copies[-1].start()
    for b in range(4):
        for head in range(8):
            high, core, h = head // 4, (head // 2) % 2, head % 2
            rows = back_ref[:, core, :, b, high, h * 16 : h * 16 + 16, :].reshape(ROWS, D)
            qs[b, :, head * D : (head + 1) * D] = dot(plan, rows).astype(jnp.bfloat16)
        far = q_hbm.at[:, pl.ds(b * 8 * D, 8 * D)]
        copies.append(pltpu.make_async_copy(qs.at[b], far, sent.at[b]))
        copies[-1].start()
    for copy in copies:
        copy.wait()


def swapped(array):
    return lax.ppermute(array, "dp", [(i, i ^ 1) for i in range(8)])


def vmem(count):
    return [pl.BlockSpec(memory_space=pltpu.VMEM)] * count


SMEM = pl.BlockSpec(memory_space=pltpu.SMEM)
PARAMS = pltpu.CompilerParams(vmem_limit_bytes=VMEM)
WIDE = pltpu.CompilerParams(vmem_limit_bytes=42 * 1024 * 1024)


def cost(flops, size):
    return pl.CostEstimate(flops=flops, bytes_accessed=size, transcendentals=0)


def take(recv):
    return pl.pallas_call(
        take_kernel,
        grid=(4,),
        in_specs=[pl.BlockSpec((32, 16, D), lambda i: (i, 4, 0))],
        out_specs=pl.BlockSpec((32, 16, D), lambda i: (i, 0, 0)),
        out_shape=jax.ShapeDtypeStruct((128, 16, D), jnp.bfloat16),
        compiler_params=PARAMS,
        name="take",
    )(recv)


def sort(info, recv):
    bf, f32 = jnp.bfloat16, jnp.float32
    return pl.pallas_call(
        sort_kernel,
        in_specs=[SMEM] + vmem(1),
        out_specs=vmem(3),
        out_shape=[
            jax.ShapeDtypeStruct((QTILES, 2 * QUERIES, D), bf),
            jax.ShapeDtypeStruct((QTILES, 2 * QUERIES, D), bf),
            jax.ShapeDtypeStruct((QTILES, 1, 2 * QUERIES), f32),
        ],
        scratch_shapes=[pltpu.VMEM((TOKENS, D), bf)],
        compiler_params=PARAMS,
        cost_estimate=cost(10**9, 6 * 10**6),
        name="sort",
    )(info, recv)


def attention(info, near, far, mine, other, q, g, delta):
    bf, f32 = jnp.bfloat16, jnp.float32
    pairs = sum(i * QUERIES // KEYS + 1 for i in range(QTILES)) + UNROLL + TAIL
    return pl.pallas_call(
        attention_kernel,
        in_specs=[SMEM] * 3 + vmem(5),
        out_specs=vmem(3),
        out_shape=[
            jax.ShapeDtypeStruct((QTILES, D, 2 * QUERIES), f32),
            jax.ShapeDtypeStruct((128, 16, D), bf),
            jax.ShapeDtypeStruct((128, 16, D), bf),
        ],
        scratch_shapes=[
            pltpu.VMEM((KTILES, KEYS, D), bf),
            pltpu.VMEM((KTILES, KEYS, D), bf),
            pltpu.VMEM((KTILES, D, KEYS), bf),
            pltpu.VMEM((pairs, KEYS, 2 * QUERIES), f32),
            pltpu.VMEM((KTILES, KEYS, D), f32),
            pltpu.VMEM((KTILES, KEYS, D), f32),
            pltpu.VMEM((QTILES, 8, 2 * QUERIES), f32),
            pltpu.SMEM((2, pairs), jnp.int32),
        ],
        compiler_params=WIDE,
        cost_estimate=cost(4 * 10**9, 10**7),
        name="attention",
    )(info, near, far, mine, other, q, g, delta)


def unsort(dq):
    return pl.pallas_call(
        unsort_kernel,
        in_specs=vmem(1),
        out_specs=vmem(1)[0],
        out_shape=jax.ShapeDtypeStruct((128, 48, D), jnp.bfloat16),
        scratch_shapes=[pltpu.VMEM((QTILES, 2 * QUERIES, D), jnp.bfloat16)],
        compiler_params=PARAMS,
        cost_estimate=cost(10**9, 4 * 10**6),
        name="unsort",
    )(dq)


def add(back, mine, other):
    part = pl.BlockSpec((32, 16, D), lambda i: (i, 0, 0))
    return pl.pallas_call(
        add_kernel,
        grid=(4,),
        in_specs=[pl.BlockSpec(memory_space=pl.ANY), part, part],
        out_specs=pl.BlockSpec((32, 16, D), lambda i: (i, 2, 0)),
        out_shape=jax.ShapeDtypeStruct((128, 48, D), jnp.bfloat16),
        input_output_aliases={0: 0},
        compiler_params=PARAMS,
        name="add",
    )(back, mine, other)


HBM = pl.BlockSpec(memory_space=pltpu.HBM)


def pack(slot, q, o, g, k, v):
    bf = jnp.bfloat16
    return pl.pallas_call(
        pack_kernel,
        in_specs=[HBM] * 6,
        out_specs=vmem(1)[0],
        out_shape=jax.ShapeDtypeStruct((*CUT, 88, D), bf),
        scratch_shapes=[pltpu.VMEM((1, ROWS), jnp.int32)]
        + [pltpu.VMEM((4, ROWS, 8 * D), bf)] * 3
        + [pltpu.VMEM((ROWS, 4 * D), bf)] * 2
        + [pltpu.SemaphoreType.DMA((15,))],
        compiler_params=pltpu.CompilerParams(vmem_limit_bytes=32 * 1024 * 1024),
        name="pack",
    )(slot, q, o, g, k, v)


def unpack(slot, back):
    bf = jnp.bfloat16
    return pl.pallas_call(
        unpack_kernel,
        in_specs=vmem(2),
        out_specs=[HBM] * 3,
        out_shape=[
            jax.ShapeDtypeStruct((ROWS, 32 * D), bf),
            jax.ShapeDtypeStruct((ROWS, 4 * D), bf),
            jax.ShapeDtypeStruct((ROWS, 4 * D), bf),
        ],
        scratch_shapes=[
            pltpu.VMEM((4, ROWS, 8 * D), bf),
            pltpu.VMEM((ROWS, 4 * D), bf),
            pltpu.VMEM((ROWS, 4 * D), bf),
            pltpu.SemaphoreType.DMA((6,)),
        ],
        compiler_params=PARAMS,
        name="unpack",
    )(slot, back)


def per_device(queries, keys, values, attn_out, out_grad, send_slot, proof_length_list):
    core = lax.axis_index("dp") & 1
    ctx = lax.axis_index("ctx")
    info = jnp.stack([core, (ctx & 1) * 2 + core, ctx >> 3 == core]).astype(jnp.int32)
    lengths = swapped(proof_length_list)

    far = [
        pltpu.with_memory_space_constraint(array, pltpu.HBM)
        for array in (send_slot, queries, attn_out, out_grad, keys, values)
    ]
    send = pack(*far)
    recv = lax.all_to_all(
        send.reshape(128, 88, D), ("dp", "ctx"), split_axis=0, concat_axis=0, tiled=True
    )
    mine = take(recv)
    other = swapped(mine)
    q, g, delta = sort(info, recv)
    dq, keep, give = attention(info, proof_length_list, lengths, mine, other, q, g, delta)
    back = add(unsort(dq), keep, swapped(give))
    back = lax.all_to_all(back, ("dp", "ctx"), split_axis=0, concat_axis=0, tiled=True)
    return unpack(send_slot, back.reshape(*CUT, 48, D))


def solution(mesh):
    rows = P(("dp", "ctx"), None)
    return jax.shard_map(
        per_device,
        mesh=mesh,
        in_specs=(rows, rows, rows, rows, rows, rows, P("dp", None)),
        out_specs=(rows, rows, rows),
        check_vma=False,
    )
```

```python
import jax
import jax.numpy as jnp
from jax import lax
from jax.experimental import pallas as pl
from jax.experimental.pallas import tpu as pltpu
from jax.sharding import PartitionSpec as P

D = 128
ROWS = 128
KEYS = 256
QUERIES = 256
TOKENS = 2048
KTILES = TOKENS // KEYS
QTILES = TOKENS // QUERIES
UNROLL = 12
TAIL = 4
AHEAD = 1
CUT = (4, 2, 2, 4, 2)
SCALE = D ** (-0.5)
LOG2E = 1.4426950408889634
VMEM = 32 * 1024 * 1024
NT = (((1,), (1,)), ((), ()))
NN = (((1,), (0,)), ((), ()))


def dot(a, b, dims=NN):
    return lax.dot_general(a, b, dims, preferred_element_type=jnp.float32)


def plan_matrix(slot_ref):
    p = lax.broadcasted_iota(jnp.int32, (ROWS, ROWS), 0)
    return (p == slot_ref[...]).astype(jnp.float32)


def pack_kernel(
    slot_hbm, q_hbm, o_hbm, g_hbm, k_hbm, v_hbm, out_ref, slot, qs, os, gs, ks, vs, arrived
):
    copies = []
    for b in range(4):
        cols = pl.ds(b * 8 * D, 8 * D)
        for n, (far, near) in enumerate(((q_hbm, qs), (g_hbm, gs), (o_hbm, os))):
            copies.append(
                pltpu.make_async_copy(far.at[:, cols], near.at[b], arrived.at[b * 3 + n])
            )
    copies.append(pltpu.make_async_copy(k_hbm, ks, arrived.at[12]))
    copies.append(pltpu.make_async_copy(v_hbm, vs, arrived.at[13]))
    first = pltpu.make_async_copy(slot_hbm, slot, arrived.at[14])
    first.start()
    for copy in copies:
        copy.start()
    first.wait()
    plan = plan_matrix(slot).astype(jnp.bfloat16)
    lane = lax.broadcasted_iota(jnp.int32, (ROWS, D), 1)

    def placed(columns):
        return dot(plan, columns).astype(jnp.bfloat16).reshape(4, 2, 16, D)

    for b in range(4):
        for copy in copies[b * 3 : b * 3 + 3]:
            copy.wait()
        delta = jnp.zeros((ROWS, D), jnp.float32)
        for head in range(8):
            high, core, h = head // 4, (head // 2) % 2, head % 2
            cols = slice(head * D, (head + 1) * D)
            g = gs[b, :, cols]
            out_ref[:, core, :, b, high, h * 16 : h * 16 + 16, :] = placed(qs[b, :, cols])
            out_ref[:, core, :, b, high, 32 + h * 16 : 48 + h * 16, :] = placed(g)
            total = jnp.sum(
                os[b, :, cols].astype(jnp.float32) * g.astype(jnp.float32), axis=1, keepdims=True
            )
            delta = jnp.where(lane == head, total, delta)
        first = delta.astype(jnp.bfloat16).astype(jnp.float32)
        second = (delta - first).astype(jnp.bfloat16).astype(jnp.float32)
        third = delta - first - second
        parts = first + pltpu.roll(second, 8, 1) + pltpu.roll(third, 16, 1)
        parts = dot(plan, parts.astype(jnp.bfloat16)).reshape(8, 16, D)
        parts = (parts[:, :8] + pltpu.roll(parts[:, 8:], 64, 2)).astype(jnp.bfloat16)
        parts = parts.reshape(4, 2, 8, D)
        for high in range(2):
            for core in range(2):
                out_ref[:, core, :, b, high, 80:88, :] = parts
    copies[12].wait()
    copies[13].wait()
    for b in range(4):
        cols = slice(b * D, (b + 1) * D)
        for core, rows in ((0, ks), (1, vs)):
            rows = placed(rows[:, cols])
            for high in range(2):
                out_ref[:, core, :, b, high, 64:80, :] = rows


def swap_matrix(bits):
    size = 16 << bits
    r = lax.broadcasted_iota(jnp.int32, (size, size), 0)
    c = lax.broadcasted_iota(jnp.int32, (size, size), 1)
    same = ((r >> 4) == (c & ((1 << bits) - 1))) & ((r & 15) == (c >> bits))
    return same.astype(jnp.float32).astype(jnp.bfloat16)


def pieces():
    for half in range(2):
        for part in range(4):
            first = half * 64 + part * 16
            yield (
                slice(first, first + 16),
                [(c if half == 0 else 31 - c) * 64 + part * 16 for c in range(16)],
            )


def take_kernel(recv_ref, out_ref):
    out_ref[...] = recv_ref[...]


def sort_kernel(info_ref, recv_ref, qs, gs, dt, ds):
    swap = swap_matrix(4)
    short = swap_matrix(3)
    for src, places in pieces():

        def rows(n):
            return recv_ref[src, n * 16 : n * 16 + 16, :].reshape(256, D)

        for n, out in ((0, qs), (2, gs)):
            both = jnp.concatenate([rows(n), rows(n + 1)], axis=1)
            both = dot(swap, both).astype(jnp.bfloat16)
            for c, at in enumerate(places):
                tile, off = at // QUERIES, at % QUERIES
                r = slice(c * 16, c * 16 + 16)
                out[tile, off : off + 16, :] = both[r, :D]
                out[tile, QUERIES + off : QUERIES + off + 16, :] = both[r, D:]
        d = recv_ref[src, 80:88, :].reshape(128, D)
        d = dot(short, d).astype(jnp.bfloat16)
        for c, at in enumerate(places):
            ds[at : at + 16, :] = d[(c % 8) * 16 : (c % 8) * 16 + 16]
    row = lax.broadcasted_iota(jnp.int32, (16, D), 0)
    lane = lax.broadcasted_iota(jnp.int32, (16, D), 1)
    pick = ((lane & 7) == info_ref[1] * 2 + row) & ((lane & 63) < 24) & (row < 2)
    for tile in range(QTILES):
        at = tile * QUERIES
        upper = int(512 <= at < 1536)
        own = (pick & (lane >> 6 == upper)).astype(jnp.float32).astype(jnp.bfloat16)
        d = dot(own, ds[at : at + QUERIES, :], NT)
        dt[tile] = jnp.concatenate([d[0:1], d[1:2]], axis=1)


def attention_kernel(
    info_ref, near_ref, far_ref, mine_ref, other_ref, qs, gs, dt, dqt, keep_ref, give_ref,
    ks, vs, kt, es, dks, dvs, sums, list_ref,
):
    core = info_ref[0]
    lengths = [jnp.where(info_ref[2] == 1, near_ref[0, n], far_ref[0, n]) for n in range(3)]
    end0 = lengths[0]
    end1 = end0 + lengths[1]
    end2 = end1 + lengths[2]

    def begin(at):
        return jnp.where(
            at >= end2, end2, jnp.where(at >= end1, end1, jnp.where(at >= end0, end0, 0))
        )

    count = jnp.int32(0)
    for i in range(QTILES):
        last = i * QUERIES // KEYS
        first = begin(jnp.int32(i * QUERIES)) // KEYS
        for j in range(last + 1):
            list_ref[0, count] = i
            list_ref[1, count] = j
            count = count + (j >= first).astype(jnp.int32)
    for extra in range(UNROLL + TAIL):
        list_ref[0, count + extra] = 0
        list_ref[1, count + extra] = KTILES - 1
    trips = (count + UNROLL // 2) // UNROLL
    rest = (jnp.maximum(count - trips * UNROLL, 0) + TAIL - 1) // TAIL

    def for_pairs(body):
        lax.fori_loop(0, trips, lambda n, c: body(n * UNROLL, UNROLL) or c, 0)
        lax.fori_loop(0, rest, lambda n, c: body(trips * UNROLL + n * TAIL, TAIL) or c, 0)

    swap = swap_matrix(4)
    for src, places in pieces():
        mine = mine_ref[src].reshape(256, D)
        other = other_ref[src].reshape(256, D)
        both = jnp.concatenate(
            [jnp.where(core == 0, mine, other), jnp.where(core == 0, other, mine)], axis=1
        )
        both = dot(swap, both).astype(jnp.bfloat16)
        for c, at in enumerate(places):
            tile, off = at // KEYS, at % KEYS
            ks[tile, off : off + 16, :] = both[c * 16 : c * 16 + 16, :D]
            vs[tile, off : off + 16, :] = both[c * 16 : c * 16 + 16, D:]
    ident = (
        lax.broadcasted_iota(jnp.int32, (D, D), 0) == lax.broadcasted_iota(jnp.int32, (D, D), 1)
    ).astype(jnp.float32).astype(jnp.bfloat16)
    for tile in range(KTILES):
        kt[tile] = dot(ident, ks[tile], NT).astype(jnp.bfloat16)
    dks[...] = jnp.zeros_like(dks)
    dvs[...] = jnp.zeros_like(dvs)
    sums[...] = jnp.zeros_like(sums)
    dqt[...] = jnp.zeros_like(dqt)

    key_row = lax.broadcasted_iota(jnp.int32, (KEYS, QUERIES), 0)
    query_lane = lax.broadcasted_iota(jnp.int32, (1, QUERIES), 1)

    def pair(n):
        return list_ref[0, n], list_ref[1, n]

    def ahead(count, start):
        begun = [start(step) for step in range(min(AHEAD, count))]
        for step in range(count):
            if step + AHEAD < count:
                begun.append(start(step + AHEAD))
            yield step, begun[step]

    def scores(first, number):
        pairs = [pair(first + step) for step in range(number)]
        made = []
        for step, s in ahead(number, lambda step: dot(ks[pairs[step][1]], qs[pairs[step][0]], NT)):
            i, j = pairs[step]
            at = i * QUERIES + query_lane
            key = key_row + j * KEYS
            seen = (key <= at) & (key >= begin(at))
            e = jnp.exp2(s * (SCALE * LOG2E))
            e = jnp.concatenate(
                [jnp.where(seen, e[:, :QUERIES], 0.0), jnp.where(seen, e[:, QUERIES:], 0.0)],
                axis=1,
            )
            es[first + step] = e
            made.append((i, jnp.sum(e.reshape(KEYS // 8, 8, 2 * QUERIES), axis=0)))
        for i, total in made:
            sums[i] += total

    for_pairs(scores)
    for i in range(QTILES):
        sums[i, 0:1, :] = 1.0 / jnp.sum(sums[i], axis=0, keepdims=True)

    def grads(first, number):
        pairs = [pair(first + step) for step in range(number)]
        made = []
        for step, dp in ahead(number, lambda step: dot(vs[pairs[step][1]], gs[pairs[step][0]], NT)):
            i, j = pairs[step]
            p = es[first + step] * sums[i, 0:1, :]
            ds = (p * (dp - dt[i])).astype(jnp.bfloat16)
            p = p.astype(jnp.bfloat16)
            made.append((i, j, dot(p, gs[i]), dot(ds, qs[i]), dot(kt[j], ds)))
        for i, j, dv, dk, dq in made:
            dvs[j] += dv
            dks[j] += dk
            dqt[i] += dq

    for_pairs(grads)
    for src, places in pieces():
        mine, other = [], []
        for at in places:
            tile, off = at // KEYS, at % KEYS
            dk = dks[tile, off : off + 16, :] * SCALE
            dv = dvs[tile, off : off + 16, :]
            mine.append(jnp.where(core == 0, dk, dv).astype(jnp.bfloat16))
            other.append(jnp.where(core == 0, dv, dk).astype(jnp.bfloat16))
        both = jnp.concatenate(
            [jnp.concatenate(mine, axis=0), jnp.concatenate(other, axis=0)], axis=1
        )
        both = dot(swap, both).astype(jnp.bfloat16)
        keep_ref[src] = both[:, :D].reshape(16, 16, D)
        give_ref[src] = both[:, D:].reshape(16, 16, D)


def unsort_kernel(dqt, back_ref, dqs):
    for i in range(QTILES):
        dqs[i] = jnp.transpose(dqt[i] * SCALE).astype(jnp.bfloat16)
    swap = swap_matrix(4)
    for src, places in pieces():
        heads = [
            jnp.concatenate(
                [
                    dqs[at // QUERIES, at % QUERIES + h * QUERIES : at % QUERIES + h * QUERIES + 16]
                    for at in places
                ],
                axis=0,
            )
            for h in range(2)
        ]
        both = dot(swap, jnp.concatenate(heads, axis=1)).astype(jnp.bfloat16)
        back_ref[src, 0:16, :] = both[:, :D].reshape(16, 16, D)
        back_ref[src, 16:32, :] = both[:, D:].reshape(16, 16, D)


def add_kernel(back_ref, mine_ref, other_ref, out_ref):
    total = mine_ref[...].astype(jnp.float32) + other_ref[...].astype(jnp.float32)
    out_ref[...] = total.astype(jnp.bfloat16)


def unpack_kernel(slot_ref, back_ref, q_hbm, k_hbm, v_hbm, qs, ks, vs, sent):
    plan = jnp.transpose(plan_matrix(slot_ref)).astype(jnp.bfloat16)
    both = jnp.concatenate([plan, plan], axis=1)
    copies = []
    for core, out in ((0, ks), (1, vs)):
        for b in range(4):
            rows = jnp.concatenate(
                [
                    back_ref[:, core, :, b, high, 32:48, :].reshape(ROWS, D)
                    for high in range(2)
                ],
                axis=0,
            )
            out[:, b * D : (b + 1) * D] = dot(both, rows).astype(jnp.bfloat16)
        far = (k_hbm, v_hbm)[core]
        copies.append(pltpu.make_async_copy(out, far, sent.at[4 + core]))
        copies[-1].start()
    for b in range(4):
        for head in range(8):
            high, core, h = head // 4, (head // 2) % 2, head % 2
            rows = back_ref[:, core, :, b, high, h * 16 : h * 16 + 16, :].reshape(ROWS, D)
            qs[b, :, head * D : (head + 1) * D] = dot(plan, rows).astype(jnp.bfloat16)
        far = q_hbm.at[:, pl.ds(b * 8 * D, 8 * D)]
        copies.append(pltpu.make_async_copy(qs.at[b], far, sent.at[b]))
        copies[-1].start()
    for copy in copies:
        copy.wait()


def swapped(array):
    return lax.ppermute(array, "dp", [(i, i ^ 1) for i in range(8)])


def vmem(count):
    return [pl.BlockSpec(memory_space=pltpu.VMEM)] * count


SMEM = pl.BlockSpec(memory_space=pltpu.SMEM)
PARAMS = pltpu.CompilerParams(vmem_limit_bytes=VMEM)
WIDE = pltpu.CompilerParams(vmem_limit_bytes=42 * 1024 * 1024)


def cost(flops, size):
    return pl.CostEstimate(flops=flops, bytes_accessed=size, transcendentals=0)


def take(recv):
    return pl.pallas_call(
        take_kernel,
        grid=(4,),
        in_specs=[pl.BlockSpec((32, 16, D), lambda i: (i, 4, 0))],
        out_specs=pl.BlockSpec((32, 16, D), lambda i: (i, 0, 0)),
        out_shape=jax.ShapeDtypeStruct((128, 16, D), jnp.bfloat16),
        compiler_params=PARAMS,
        name="take",
    )(recv)


def sort(info, recv):
    bf, f32 = jnp.bfloat16, jnp.float32
    return pl.pallas_call(
        sort_kernel,
        in_specs=[SMEM] + vmem(1),
        out_specs=vmem(3),
        out_shape=[
            jax.ShapeDtypeStruct((QTILES, 2 * QUERIES, D), bf),
            jax.ShapeDtypeStruct((QTILES, 2 * QUERIES, D), bf),
            jax.ShapeDtypeStruct((QTILES, 1, 2 * QUERIES), f32),
        ],
        scratch_shapes=[pltpu.VMEM((TOKENS, D), bf)],
        compiler_params=PARAMS,
        cost_estimate=cost(10**9, 6 * 10**6),
        name="sort",
    )(info, recv)


def attention(info, near, far, mine, other, q, g, delta):
    bf, f32 = jnp.bfloat16, jnp.float32
    pairs = sum(i * QUERIES // KEYS + 1 for i in range(QTILES)) + UNROLL + TAIL
    return pl.pallas_call(
        attention_kernel,
        in_specs=[SMEM] * 3 + vmem(5),
        out_specs=vmem(3),
        out_shape=[
            jax.ShapeDtypeStruct((QTILES, D, 2 * QUERIES), f32),
            jax.ShapeDtypeStruct((128, 16, D), bf),
            jax.ShapeDtypeStruct((128, 16, D), bf),
        ],
        scratch_shapes=[
            pltpu.VMEM((KTILES, KEYS, D), bf),
            pltpu.VMEM((KTILES, KEYS, D), bf),
            pltpu.VMEM((KTILES, D, KEYS), bf),
            pltpu.VMEM((pairs, KEYS, 2 * QUERIES), f32),
            pltpu.VMEM((KTILES, KEYS, D), f32),
            pltpu.VMEM((KTILES, KEYS, D), f32),
            pltpu.VMEM((QTILES, 8, 2 * QUERIES), f32),
            pltpu.SMEM((2, pairs), jnp.int32),
        ],
        compiler_params=WIDE,
        cost_estimate=cost(4 * 10**9, 10**7),
        name="attention",
    )(info, near, far, mine, other, q, g, delta)


def unsort(dq):
    return pl.pallas_call(
        unsort_kernel,
        in_specs=vmem(1),
        out_specs=vmem(1)[0],
        out_shape=jax.ShapeDtypeStruct((128, 48, D), jnp.bfloat16),
        scratch_shapes=[pltpu.VMEM((QTILES, 2 * QUERIES, D), jnp.bfloat16)],
        compiler_params=PARAMS,
        cost_estimate=cost(10**9, 4 * 10**6),
        name="unsort",
    )(dq)


def add(back, mine, other):
    part = pl.BlockSpec((32, 16, D), lambda i: (i, 0, 0))
    return pl.pallas_call(
        add_kernel,
        grid=(4,),
        in_specs=[pl.BlockSpec(memory_space=pl.ANY), part, part],
        out_specs=pl.BlockSpec((32, 16, D), lambda i: (i, 2, 0)),
        out_shape=jax.ShapeDtypeStruct((128, 48, D), jnp.bfloat16),
        input_output_aliases={0: 0},
        compiler_params=PARAMS,
        name="add",
    )(back, mine, other)


HBM = pl.BlockSpec(memory_space=pltpu.HBM)


def pack(slot, q, o, g, k, v):
    bf = jnp.bfloat16
    return pl.pallas_call(
        pack_kernel,
        in_specs=[HBM] * 6,
        out_specs=vmem(1)[0],
        out_shape=jax.ShapeDtypeStruct((*CUT, 88, D), bf),
        scratch_shapes=[pltpu.VMEM((1, ROWS), jnp.int32)]
        + [pltpu.VMEM((4, ROWS, 8 * D), bf)] * 3
        + [pltpu.VMEM((ROWS, 4 * D), bf)] * 2
        + [pltpu.SemaphoreType.DMA((15,))],
        compiler_params=pltpu.CompilerParams(vmem_limit_bytes=32 * 1024 * 1024),
        name="pack",
    )(slot, q, o, g, k, v)


def unpack(slot, back):
    bf = jnp.bfloat16
    return pl.pallas_call(
        unpack_kernel,
        in_specs=vmem(2),
        out_specs=[HBM] * 3,
        out_shape=[
            jax.ShapeDtypeStruct((ROWS, 32 * D), bf),
            jax.ShapeDtypeStruct((ROWS, 4 * D), bf),
            jax.ShapeDtypeStruct((ROWS, 4 * D), bf),
        ],
        scratch_shapes=[
            pltpu.VMEM((4, ROWS, 8 * D), bf),
            pltpu.VMEM((ROWS, 4 * D), bf),
            pltpu.VMEM((ROWS, 4 * D), bf),
            pltpu.SemaphoreType.DMA((6,)),
        ],
        compiler_params=PARAMS,
        name="unpack",
    )(slot, back)


def per_device(queries, keys, values, attn_out, out_grad, send_slot, proof_length_list):
    core = lax.axis_index("dp") & 1
    ctx = lax.axis_index("ctx")
    info = jnp.stack([core, (ctx & 1) * 2 + core, ctx >> 3 == core]).astype(jnp.int32)
    lengths = swapped(proof_length_list)

    far = [
        pltpu.with_memory_space_constraint(array, pltpu.HBM)
        for array in (send_slot, queries, attn_out, out_grad, keys, values)
    ]
    send, lengths = lax.optimization_barrier((pack(*far), lengths))
    recv = lax.all_to_all(
        send.reshape(128, 88, D), ("dp", "ctx"), split_axis=0, concat_axis=0, tiled=True
    )
    mine = take(recv)
    other = swapped(mine)
    q, g, delta = sort(info, recv)
    dq, keep, give = attention(info, proof_length_list, lengths, mine, other, q, g, delta)
    back = add(unsort(dq), keep, swapped(give))
    back = lax.all_to_all(back, ("dp", "ctx"), split_axis=0, concat_axis=0, tiled=True)
    return unpack(send_slot, back.reshape(*CUT, 48, D))


def solution(mesh):
    rows = P(("dp", "ctx"), None)
    return jax.shard_map(
        per_device,
        mesh=mesh,
        in_specs=(rows, rows, rows, rows, rows, rows, P("dp", None)),
        out_specs=(rows, rows, rows),
        check_vma=False,
    )
```

```python
import jax
import jax.numpy as jnp
from jax import lax
from jax.experimental import pallas as pl
from jax.experimental.pallas import tpu as pltpu
from jax.sharding import PartitionSpec as P

D = 128
ROWS = 128
KEYS = 256
QUERIES = 256
TOKENS = 2048
KTILES = TOKENS // KEYS
QTILES = TOKENS // QUERIES
UNROLL = 24
TAIL = 4
AHEAD = 1
CUT = (4, 2, 2, 4, 2)
SCALE = D ** (-0.5)
LOG2E = 1.4426950408889634
VMEM = 32 * 1024 * 1024
NT = (((1,), (1,)), ((), ()))
NN = (((1,), (0,)), ((), ()))


def dot(a, b, dims=NN):
    return lax.dot_general(a, b, dims, preferred_element_type=jnp.float32)


def plan_matrix(slot_ref):
    p = lax.broadcasted_iota(jnp.int32, (ROWS, ROWS), 0)
    return (p == slot_ref[...]).astype(jnp.float32)


def pack_kernel(
    slot_hbm, q_hbm, o_hbm, g_hbm, k_hbm, v_hbm, out_ref, slot, qs, os, gs, ks, vs, arrived
):
    copies = []
    for b in range(4):
        cols = pl.ds(b * 8 * D, 8 * D)
        for n, (far, near) in enumerate(((q_hbm, qs), (g_hbm, gs), (o_hbm, os))):
            copies.append(
                pltpu.make_async_copy(far.at[:, cols], near.at[b], arrived.at[b * 3 + n])
            )
    copies.append(pltpu.make_async_copy(k_hbm, ks, arrived.at[12]))
    copies.append(pltpu.make_async_copy(v_hbm, vs, arrived.at[13]))
    first = pltpu.make_async_copy(slot_hbm, slot, arrived.at[14])
    first.start()
    for copy in copies:
        copy.start()
    first.wait()
    plan = plan_matrix(slot).astype(jnp.bfloat16)
    lane = lax.broadcasted_iota(jnp.int32, (ROWS, D), 1)

    def placed(columns):
        return dot(plan, columns).astype(jnp.bfloat16).reshape(4, 2, 16, D)

    for b in range(4):
        for copy in copies[b * 3 : b * 3 + 3]:
            copy.wait()
        delta = jnp.zeros((ROWS, D), jnp.float32)
        for head in range(8):
            high, core, h = head // 4, (head // 2) % 2, head % 2
            cols = slice(head * D, (head + 1) * D)
            g = gs[b, :, cols]
            out_ref[:, core, :, b, high, h * 16 : h * 16 + 16, :] = placed(qs[b, :, cols])
            out_ref[:, core, :, b, high, 32 + h * 16 : 48 + h * 16, :] = placed(g)
            total = jnp.sum(
                os[b, :, cols].astype(jnp.float32) * g.astype(jnp.float32), axis=1, keepdims=True
            )
            delta = jnp.where(lane == head, total, delta)
        first = delta.astype(jnp.bfloat16).astype(jnp.float32)
        second = (delta - first).astype(jnp.bfloat16).astype(jnp.float32)
        third = delta - first - second
        parts = first + pltpu.roll(second, 8, 1) + pltpu.roll(third, 16, 1)
        parts = dot(plan, parts.astype(jnp.bfloat16)).reshape(8, 16, D)
        parts = (parts[:, :8] + pltpu.roll(parts[:, 8:], 64, 2)).astype(jnp.bfloat16)
        parts = parts.reshape(4, 2, 8, D)
        for high in range(2):
            for core in range(2):
                out_ref[:, core, :, b, high, 80:88, :] = parts
    copies[12].wait()
    copies[13].wait()
    for b in range(4):
        cols = slice(b * D, (b + 1) * D)
        for core, rows in ((0, ks), (1, vs)):
            rows = placed(rows[:, cols])
            for high in range(2):
                out_ref[:, core, :, b, high, 64:80, :] = rows


def swap_matrix(bits):
    size = 16 << bits
    r = lax.broadcasted_iota(jnp.int32, (size, size), 0)
    c = lax.broadcasted_iota(jnp.int32, (size, size), 1)
    same = ((r >> 4) == (c & ((1 << bits) - 1))) & ((r & 15) == (c >> bits))
    return same.astype(jnp.float32).astype(jnp.bfloat16)


def pieces():
    for half in range(2):
        for part in range(4):
            first = half * 64 + part * 16
            yield (
                slice(first, first + 16),
                [(c if half == 0 else 31 - c) * 64 + part * 16 for c in range(16)],
            )


def take_kernel(recv_ref, out_ref):
    out_ref[...] = recv_ref[...]


def sort_kernel(info_ref, recv_ref, qs, gs, dt, ds):
    swap = swap_matrix(4)
    short = swap_matrix(3)
    for src, places in pieces():

        def rows(n):
            return recv_ref[src, n * 16 : n * 16 + 16, :].reshape(256, D)

        for n, out in ((0, qs), (2, gs)):
            both = jnp.concatenate([rows(n), rows(n + 1)], axis=1)
            both = dot(swap, both).astype(jnp.bfloat16)
            for c, at in enumerate(places):
                tile, off = at // QUERIES, at % QUERIES
                r = slice(c * 16, c * 16 + 16)
                out[tile, off : off + 16, :] = both[r, :D]
                out[tile, QUERIES + off : QUERIES + off + 16, :] = both[r, D:]
        d = recv_ref[src, 80:88, :].reshape(128, D)
        d = dot(short, d).astype(jnp.bfloat16)
        for c, at in enumerate(places):
            ds[at : at + 16, :] = d[(c % 8) * 16 : (c % 8) * 16 + 16]
    row = lax.broadcasted_iota(jnp.int32, (16, D), 0)
    lane = lax.broadcasted_iota(jnp.int32, (16, D), 1)
    pick = ((lane & 7) == info_ref[1] * 2 + row) & ((lane & 63) < 24) & (row < 2)
    for tile in range(QTILES):
        at = tile * QUERIES
        upper = int(512 <= at < 1536)
        own = (pick & (lane >> 6 == upper)).astype(jnp.float32).astype(jnp.bfloat16)
        d = dot(own, ds[at : at + QUERIES, :], NT)
        dt[tile] = jnp.concatenate([d[0:1], d[1:2]], axis=1)


def attention_kernel(
    info_ref, near_ref, far_ref, mine_ref, other_ref, qs, gs, dt, dqt, keep_ref, give_ref,
    ks, vs, kt, es, dks, dvs, sums, list_ref,
):
    core = info_ref[0]
    lengths = [jnp.where(info_ref[2] == 1, near_ref[0, n], far_ref[0, n]) for n in range(3)]
    end0 = lengths[0]
    end1 = end0 + lengths[1]
    end2 = end1 + lengths[2]

    def begin(at):
        return jnp.where(
            at >= end2, end2, jnp.where(at >= end1, end1, jnp.where(at >= end0, end0, 0))
        )

    count = jnp.int32(0)
    for i in range(QTILES):
        last = i * QUERIES // KEYS
        first = begin(jnp.int32(i * QUERIES)) // KEYS
        for j in range(last + 1):
            list_ref[0, count] = i
            list_ref[1, count] = j
            count = count + (j >= first).astype(jnp.int32)
    for extra in range(UNROLL + TAIL):
        list_ref[0, count + extra] = 0
        list_ref[1, count + extra] = KTILES - 1
    trips = (count + UNROLL // 2) // UNROLL
    rest = (jnp.maximum(count - trips * UNROLL, 0) + TAIL - 1) // TAIL

    def for_pairs(body):
        lax.fori_loop(0, trips, lambda n, c: body(n * UNROLL, UNROLL) or c, 0)
        lax.fori_loop(0, rest, lambda n, c: body(trips * UNROLL + n * TAIL, TAIL) or c, 0)

    swap = swap_matrix(4)
    for src, places in pieces():
        mine = mine_ref[src].reshape(256, D)
        other = other_ref[src].reshape(256, D)
        both = jnp.concatenate(
            [jnp.where(core == 0, mine, other), jnp.where(core == 0, other, mine)], axis=1
        )
        both = dot(swap, both).astype(jnp.bfloat16)
        for c, at in enumerate(places):
            tile, off = at // KEYS, at % KEYS
            ks[tile, off : off + 16, :] = both[c * 16 : c * 16 + 16, :D]
            vs[tile, off : off + 16, :] = both[c * 16 : c * 16 + 16, D:]
    ident = (
        lax.broadcasted_iota(jnp.int32, (D, D), 0) == lax.broadcasted_iota(jnp.int32, (D, D), 1)
    ).astype(jnp.float32).astype(jnp.bfloat16)
    for tile in range(KTILES):
        kt[tile] = dot(ident, ks[tile], NT).astype(jnp.bfloat16)
    dks[...] = jnp.zeros_like(dks)
    dvs[...] = jnp.zeros_like(dvs)
    sums[...] = jnp.zeros_like(sums)
    dqt[...] = jnp.zeros_like(dqt)

    key_row = lax.broadcasted_iota(jnp.int32, (KEYS, QUERIES), 0)
    query_lane = lax.broadcasted_iota(jnp.int32, (1, QUERIES), 1)

    def pair(n):
        return list_ref[0, n], list_ref[1, n]

    def ahead(count, start):
        begun = [start(step) for step in range(min(AHEAD, count))]
        for step in range(count):
            if step + AHEAD < count:
                begun.append(start(step + AHEAD))
            yield step, begun[step]

    def scores(first, number):
        pairs = [pair(first + step) for step in range(number)]
        made = []
        for step, s in ahead(number, lambda step: dot(ks[pairs[step][1]], qs[pairs[step][0]], NT)):
            i, j = pairs[step]
            at = i * QUERIES + query_lane
            key = key_row + j * KEYS
            seen = (key <= at) & (key >= begin(at))
            e = jnp.exp2(s * (SCALE * LOG2E))
            e = jnp.concatenate(
                [jnp.where(seen, e[:, :QUERIES], 0.0), jnp.where(seen, e[:, QUERIES:], 0.0)],
                axis=1,
            )
            es[first + step] = e
            made.append((i, jnp.sum(e.reshape(KEYS // 8, 8, 2 * QUERIES), axis=0)))
        for i, total in made:
            sums[i] += total

    for_pairs(scores)
    for i in range(QTILES):
        sums[i, 0:1, :] = 1.0 / jnp.sum(sums[i], axis=0, keepdims=True)

    def grads(first, number):
        pairs = [pair(first + step) for step in range(number)]
        made = []
        for step, dp in ahead(number, lambda step: dot(vs[pairs[step][1]], gs[pairs[step][0]], NT)):
            i, j = pairs[step]
            p = es[first + step] * sums[i, 0:1, :]
            ds = (p * (dp - dt[i])).astype(jnp.bfloat16)
            p = p.astype(jnp.bfloat16)
            made.append((i, j, dot(p, gs[i]), dot(ds, qs[i]), dot(kt[j], ds)))
        for i, j, dv, dk, dq in made:
            dvs[j] += dv
            dks[j] += dk
            dqt[i] += dq

    for_pairs(grads)
    for src, places in pieces():
        mine, other = [], []
        for at in places:
            tile, off = at // KEYS, at % KEYS
            dk = dks[tile, off : off + 16, :] * SCALE
            dv = dvs[tile, off : off + 16, :]
            mine.append(jnp.where(core == 0, dk, dv).astype(jnp.bfloat16))
            other.append(jnp.where(core == 0, dv, dk).astype(jnp.bfloat16))
        both = jnp.concatenate(
            [jnp.concatenate(mine, axis=0), jnp.concatenate(other, axis=0)], axis=1
        )
        both = dot(swap, both).astype(jnp.bfloat16)
        keep_ref[src] = both[:, :D].reshape(16, 16, D)
        give_ref[src] = both[:, D:].reshape(16, 16, D)


def unsort_kernel(dqt, back_ref, dqs):
    for i in range(QTILES):
        dqs[i] = jnp.transpose(dqt[i] * SCALE).astype(jnp.bfloat16)
    swap = swap_matrix(4)
    for src, places in pieces():
        heads = [
            jnp.concatenate(
                [
                    dqs[at // QUERIES, at % QUERIES + h * QUERIES : at % QUERIES + h * QUERIES + 16]
                    for at in places
                ],
                axis=0,
            )
            for h in range(2)
        ]
        both = dot(swap, jnp.concatenate(heads, axis=1)).astype(jnp.bfloat16)
        back_ref[src, 0:16, :] = both[:, :D].reshape(16, 16, D)
        back_ref[src, 16:32, :] = both[:, D:].reshape(16, 16, D)


def add_kernel(back_ref, mine_ref, other_ref, out_ref):
    total = mine_ref[...].astype(jnp.float32) + other_ref[...].astype(jnp.float32)
    out_ref[...] = total.astype(jnp.bfloat16)


def unpack_kernel(slot_ref, back_ref, q_hbm, k_hbm, v_hbm, qs, ks, vs, sent):
    plan = jnp.transpose(plan_matrix(slot_ref)).astype(jnp.bfloat16)
    both = jnp.concatenate([plan, plan], axis=1)
    copies = []
    for core, out in ((0, ks), (1, vs)):
        for b in range(4):
            rows = jnp.concatenate(
                [
                    back_ref[:, core, :, b, high, 32:48, :].reshape(ROWS, D)
                    for high in range(2)
                ],
                axis=0,
            )
            out[:, b * D : (b + 1) * D] = dot(both, rows).astype(jnp.bfloat16)
        far = (k_hbm, v_hbm)[core]
        copies.append(pltpu.make_async_copy(out, far, sent.at[4 + core]))
        copies[-1].start()
    for b in range(4):
        for head in range(8):
            high, core, h = head // 4, (head // 2) % 2, head % 2
            rows = back_ref[:, core, :, b, high, h * 16 : h * 16 + 16, :].reshape(ROWS, D)
            qs[b, :, head * D : (head + 1) * D] = dot(plan, rows).astype(jnp.bfloat16)
        far = q_hbm.at[:, pl.ds(b * 8 * D, 8 * D)]
        copies.append(pltpu.make_async_copy(qs.at[b], far, sent.at[b]))
        copies[-1].start()
    for copy in copies:
        copy.wait()


def swapped(array):
    return lax.ppermute(array, "dp", [(i, i ^ 1) for i in range(8)])


def vmem(count):
    return [pl.BlockSpec(memory_space=pltpu.VMEM)] * count


SMEM = pl.BlockSpec(memory_space=pltpu.SMEM)
PARAMS = pltpu.CompilerParams(vmem_limit_bytes=VMEM)
WIDE = pltpu.CompilerParams(vmem_limit_bytes=42 * 1024 * 1024)


def cost(flops, size):
    return pl.CostEstimate(flops=flops, bytes_accessed=size, transcendentals=0)


def take(recv):
    return pl.pallas_call(
        take_kernel,
        grid=(4,),
        in_specs=[pl.BlockSpec((32, 16, D), lambda i: (i, 4, 0))],
        out_specs=pl.BlockSpec((32, 16, D), lambda i: (i, 0, 0)),
        out_shape=jax.ShapeDtypeStruct((128, 16, D), jnp.bfloat16),
        compiler_params=PARAMS,
        name="take",
    )(recv)


def sort(info, recv):
    bf, f32 = jnp.bfloat16, jnp.float32
    return pl.pallas_call(
        sort_kernel,
        in_specs=[SMEM] + vmem(1),
        out_specs=vmem(3),
        out_shape=[
            jax.ShapeDtypeStruct((QTILES, 2 * QUERIES, D), bf),
            jax.ShapeDtypeStruct((QTILES, 2 * QUERIES, D), bf),
            jax.ShapeDtypeStruct((QTILES, 1, 2 * QUERIES), f32),
        ],
        scratch_shapes=[pltpu.VMEM((TOKENS, D), bf)],
        compiler_params=PARAMS,
        cost_estimate=cost(10**9, 6 * 10**6),
        name="sort",
    )(info, recv)


def attention(info, near, far, mine, other, q, g, delta):
    bf, f32 = jnp.bfloat16, jnp.float32
    most = sum(i * QUERIES // KEYS + 1 for i in range(QTILES))
    kept = max(pl.cdiv(most, UNROLL) * UNROLL, most + TAIL)
    return pl.pallas_call(
        attention_kernel,
        in_specs=[SMEM] * 3 + vmem(5),
        out_specs=vmem(3),
        out_shape=[
            jax.ShapeDtypeStruct((QTILES, D, 2 * QUERIES), f32),
            jax.ShapeDtypeStruct((128, 16, D), bf),
            jax.ShapeDtypeStruct((128, 16, D), bf),
        ],
        scratch_shapes=[
            pltpu.VMEM((KTILES, KEYS, D), bf),
            pltpu.VMEM((KTILES, KEYS, D), bf),
            pltpu.VMEM((KTILES, D, KEYS), bf),
            pltpu.VMEM((kept, KEYS, 2 * QUERIES), f32),
            pltpu.VMEM((KTILES, KEYS, D), f32),
            pltpu.VMEM((KTILES, KEYS, D), f32),
            pltpu.VMEM((QTILES, 8, 2 * QUERIES), f32),
            pltpu.SMEM((2, most + UNROLL + TAIL), jnp.int32),
        ],
        compiler_params=WIDE,
        cost_estimate=cost(4 * 10**9, 10**7),
        name="attention",
    )(info, near, far, mine, other, q, g, delta)


def unsort(dq):
    return pl.pallas_call(
        unsort_kernel,
        in_specs=vmem(1),
        out_specs=vmem(1)[0],
        out_shape=jax.ShapeDtypeStruct((128, 48, D), jnp.bfloat16),
        scratch_shapes=[pltpu.VMEM((QTILES, 2 * QUERIES, D), jnp.bfloat16)],
        compiler_params=PARAMS,
        cost_estimate=cost(10**9, 4 * 10**6),
        name="unsort",
    )(dq)


def add(back, mine, other):
    part = pl.BlockSpec((32, 16, D), lambda i: (i, 0, 0))
    return pl.pallas_call(
        add_kernel,
        grid=(4,),
        in_specs=[pl.BlockSpec(memory_space=pl.ANY), part, part],
        out_specs=pl.BlockSpec((32, 16, D), lambda i: (i, 2, 0)),
        out_shape=jax.ShapeDtypeStruct((128, 48, D), jnp.bfloat16),
        input_output_aliases={0: 0},
        compiler_params=PARAMS,
        name="add",
    )(back, mine, other)


HBM = pl.BlockSpec(memory_space=pltpu.HBM)


def pack(slot, q, o, g, k, v):
    bf = jnp.bfloat16
    return pl.pallas_call(
        pack_kernel,
        in_specs=[HBM] * 6,
        out_specs=vmem(1)[0],
        out_shape=jax.ShapeDtypeStruct((*CUT, 88, D), bf),
        scratch_shapes=[pltpu.VMEM((1, ROWS), jnp.int32)]
        + [pltpu.VMEM((4, ROWS, 8 * D), bf)] * 3
        + [pltpu.VMEM((ROWS, 4 * D), bf)] * 2
        + [pltpu.SemaphoreType.DMA((15,))],
        compiler_params=pltpu.CompilerParams(vmem_limit_bytes=32 * 1024 * 1024),
        name="pack",
    )(slot, q, o, g, k, v)


def unpack(slot, back):
    bf = jnp.bfloat16
    return pl.pallas_call(
        unpack_kernel,
        in_specs=vmem(2),
        out_specs=[HBM] * 3,
        out_shape=[
            jax.ShapeDtypeStruct((ROWS, 32 * D), bf),
            jax.ShapeDtypeStruct((ROWS, 4 * D), bf),
            jax.ShapeDtypeStruct((ROWS, 4 * D), bf),
        ],
        scratch_shapes=[
            pltpu.VMEM((4, ROWS, 8 * D), bf),
            pltpu.VMEM((ROWS, 4 * D), bf),
            pltpu.VMEM((ROWS, 4 * D), bf),
            pltpu.SemaphoreType.DMA((6,)),
        ],
        compiler_params=PARAMS,
        name="unpack",
    )(slot, back)


def per_device(queries, keys, values, attn_out, out_grad, send_slot, proof_length_list):
    core = lax.axis_index("dp") & 1
    ctx = lax.axis_index("ctx")
    info = jnp.stack([core, (ctx & 1) * 2 + core, ctx >> 3 == core]).astype(jnp.int32)
    lengths = swapped(proof_length_list)

    far = [
        pltpu.with_memory_space_constraint(array, pltpu.HBM)
        for array in (send_slot, queries, attn_out, out_grad, keys, values)
    ]
    send, lengths = lax.optimization_barrier((pack(*far), lengths))
    recv = lax.all_to_all(
        send.reshape(128, 88, D), ("dp", "ctx"), split_axis=0, concat_axis=0, tiled=True
    )
    mine = take(recv)
    other = swapped(mine)
    q, g, delta = sort(info, recv)
    dq, keep, give = attention(info, proof_length_list, lengths, mine, other, q, g, delta)
    back = add(unsort(dq), keep, swapped(give))
    back = lax.all_to_all(back, ("dp", "ctx"), split_axis=0, concat_axis=0, tiled=True)
    return unpack(send_slot, back.reshape(*CUT, 48, D))


def solution(mesh):
    rows = P(("dp", "ctx"), None)
    return jax.shard_map(
        per_device,
        mesh=mesh,
        in_specs=(rows, rows, rows, rows, rows, rows, P("dp", None)),
        out_specs=(rows, rows, rows),
        check_vma=False,
    )
```

```python
import jax
import jax.numpy as jnp
from jax import lax
from jax.experimental import pallas as pl
from jax.experimental.pallas import tpu as pltpu
from jax.sharding import PartitionSpec as P

D = 128
ROWS = 128
KEYS = 256
QUERIES = 256
TOKENS = 2048
KTILES = TOKENS // KEYS
QTILES = TOKENS // QUERIES
UNROLL = 24
TAIL = 4
AHEAD = 1
CUT = (4, 2, 2, 4, 2)
SCALE = D ** (-0.5)
LOG2E = 1.4426950408889634
VMEM = 32 * 1024 * 1024
NT = (((1,), (1,)), ((), ()))
NN = (((1,), (0,)), ((), ()))


def dot(a, b, dims=NN):
    return lax.dot_general(a, b, dims, preferred_element_type=jnp.float32)


def plan_matrix(slot_ref):
    p = lax.broadcasted_iota(jnp.int32, (ROWS, ROWS), 0)
    return (p == slot_ref[...]).astype(jnp.float32)


def pack_kernel(
    slot_hbm, q_hbm, o_hbm, g_hbm, k_hbm, v_hbm, out_ref, slot, qs, os, gs, ks, vs, arrived
):
    copies = []
    for b in range(4):
        cols = pl.ds(b * 8 * D, 8 * D)
        for n, (far, near) in enumerate(((q_hbm, qs), (g_hbm, gs), (o_hbm, os))):
            copies.append(
                pltpu.make_async_copy(far.at[:, cols], near.at[b], arrived.at[b * 3 + n])
            )
    copies.append(pltpu.make_async_copy(k_hbm, ks, arrived.at[12]))
    copies.append(pltpu.make_async_copy(v_hbm, vs, arrived.at[13]))
    first = pltpu.make_async_copy(slot_hbm, slot, arrived.at[14])
    first.start()
    for copy in copies:
        copy.start()
    first.wait()
    plan = plan_matrix(slot).astype(jnp.bfloat16)
    lane = lax.broadcasted_iota(jnp.int32, (ROWS, D), 1)

    def placed(columns):
        return dot(plan, columns).astype(jnp.bfloat16).reshape(4, 2, 16, D)

    for b in range(4):
        for copy in copies[b * 3 : b * 3 + 3]:
            copy.wait()
        delta = jnp.zeros((ROWS, D), jnp.float32)
        for head in range(8):
            high, core, h = head // 4, (head // 2) % 2, head % 2
            cols = slice(head * D, (head + 1) * D)
            g = gs[b, :, cols]
            out_ref[:, core, :, b, high, h * 16 : h * 16 + 16, :] = placed(qs[b, :, cols])
            out_ref[:, core, :, b, high, 32 + h * 16 : 48 + h * 16, :] = placed(g)
            total = jnp.sum(
                os[b, :, cols].astype(jnp.float32) * g.astype(jnp.float32), axis=1, keepdims=True
            )
            delta = jnp.where(lane == head, total, delta)
        first = delta.astype(jnp.bfloat16).astype(jnp.float32)
        second = (delta - first).astype(jnp.bfloat16).astype(jnp.float32)
        third = delta - first - second
        parts = first + pltpu.roll(second, 8, 1) + pltpu.roll(third, 16, 1)
        parts = dot(plan, parts.astype(jnp.bfloat16)).reshape(8, 16, D)
        parts = (parts[:, :8] + pltpu.roll(parts[:, 8:], 64, 2)).astype(jnp.bfloat16)
        parts = parts.reshape(4, 2, 8, D)
        for high in range(2):
            for core in range(2):
                out_ref[:, core, :, b, high, 80:88, :] = parts
    copies[12].wait()
    copies[13].wait()
    for b in range(4):
        cols = slice(b * D, (b + 1) * D)
        for core, rows in ((0, ks), (1, vs)):
            rows = placed(rows[:, cols])
            for high in range(2):
                out_ref[:, core, :, b, high, 64:80, :] = rows


def swap_matrix(bits):
    size = 16 << bits
    r = lax.broadcasted_iota(jnp.int32, (size, size), 0)
    c = lax.broadcasted_iota(jnp.int32, (size, size), 1)
    same = ((r >> 4) == (c & ((1 << bits) - 1))) & ((r & 15) == (c >> bits))
    return same.astype(jnp.float32).astype(jnp.bfloat16)


def pieces():
    for half in range(2):
        for part in range(4):
            first = half * 64 + part * 16
            yield (
                slice(first, first + 16),
                [(c if half == 0 else 31 - c) * 64 + part * 16 for c in range(16)],
            )


def take_kernel(recv_ref, out_ref):
    out_ref[...] = recv_ref[...]


def sort_kernel(info_ref, recv_ref, qs, gs, dt, ds):
    swap = swap_matrix(4)
    short = swap_matrix(3)
    for src, places in pieces():

        def rows(n):
            return recv_ref[src, n * 16 : n * 16 + 16, :].reshape(256, D)

        for n, out in ((0, qs), (2, gs)):
            both = jnp.concatenate([rows(n), rows(n + 1)], axis=1)
            both = dot(swap, both).astype(jnp.bfloat16)
            for c, at in enumerate(places):
                tile, off = at // QUERIES, at % QUERIES
                r = slice(c * 16, c * 16 + 16)
                out[tile, off : off + 16, :] = both[r, :D]
                out[tile, QUERIES + off : QUERIES + off + 16, :] = both[r, D:]
        d = recv_ref[src, 80:88, :].reshape(128, D)
        d = dot(short, d).astype(jnp.bfloat16)
        for c, at in enumerate(places):
            ds[at : at + 16, :] = d[(c % 8) * 16 : (c % 8) * 16 + 16]
    row = lax.broadcasted_iota(jnp.int32, (16, D), 0)
    lane = lax.broadcasted_iota(jnp.int32, (16, D), 1)
    pick = ((lane & 7) == info_ref[1] * 2 + row) & ((lane & 63) < 24) & (row < 2)
    for tile in range(QTILES):
        at = tile * QUERIES
        upper = int(512 <= at < 1536)
        own = (pick & (lane >> 6 == upper)).astype(jnp.float32).astype(jnp.bfloat16)
        d = dot(own, ds[at : at + QUERIES, :], NT)
        dt[tile] = jnp.concatenate([d[0:1], d[1:2]], axis=1)


def attention_kernel(
    info_ref, near_ref, far_ref, mine_ref, other_ref, qs, gs, dt, dqt, keep_ref, give_ref,
    ks, vs, kt, es, dks, dvs, sums, list_ref,
):
    core = info_ref[0]
    lengths = [jnp.where(info_ref[2] == 1, near_ref[0, n], far_ref[0, n]) for n in range(3)]
    end0 = lengths[0]
    end1 = end0 + lengths[1]
    end2 = end1 + lengths[2]

    def begin(at):
        return jnp.where(
            at >= end2, end2, jnp.where(at >= end1, end1, jnp.where(at >= end0, end0, 0))
        )

    count = jnp.int32(0)
    for i in range(QTILES):
        last = i * QUERIES // KEYS
        first = begin(jnp.int32(i * QUERIES)) // KEYS
        for j in range(last + 1):
            list_ref[0, count] = i
            list_ref[1, count] = j
            count = count + (j >= first).astype(jnp.int32)
    for extra in range(UNROLL + TAIL):
        list_ref[0, count + extra] = 0
        list_ref[1, count + extra] = KTILES - 1
    trips = (count + UNROLL // 2) // UNROLL
    rest = (jnp.maximum(count - trips * UNROLL, 0) + TAIL - 1) // TAIL

    def for_pairs(body):
        lax.fori_loop(0, trips, lambda n, c: body(n * UNROLL, UNROLL) or c, 0)
        lax.fori_loop(0, rest, lambda n, c: body(trips * UNROLL + n * TAIL, TAIL) or c, 0)

    swap = swap_matrix(4)
    for src, places in pieces():
        mine = mine_ref[src].reshape(256, D)
        other = other_ref[src].reshape(256, D)
        both = jnp.concatenate(
            [jnp.where(core == 0, mine, other), jnp.where(core == 0, other, mine)], axis=1
        )
        both = dot(swap, both).astype(jnp.bfloat16)
        for c, at in enumerate(places):
            tile, off = at // KEYS, at % KEYS
            ks[tile, off : off + 16, :] = both[c * 16 : c * 16 + 16, :D]
            vs[tile, off : off + 16, :] = both[c * 16 : c * 16 + 16, D:]
    ident = (
        lax.broadcasted_iota(jnp.int32, (D, D), 0) == lax.broadcasted_iota(jnp.int32, (D, D), 1)
    ).astype(jnp.float32).astype(jnp.bfloat16)
    for tile in range(KTILES):
        kt[tile] = dot(ident, ks[tile], NT).astype(jnp.bfloat16)
    dks[...] = jnp.zeros_like(dks)
    dvs[...] = jnp.zeros_like(dvs)
    sums[...] = jnp.zeros_like(sums)
    dqt[...] = jnp.zeros_like(dqt)

    key_row = lax.broadcasted_iota(jnp.int32, (KEYS, QUERIES), 0)
    query_lane = lax.broadcasted_iota(jnp.int32, (1, QUERIES), 1)

    def pair(n):
        return list_ref[0, n], list_ref[1, n]

    def ahead(count, start):
        begun = [start(step) for step in range(min(AHEAD, count))]
        for step in range(count):
            if step + AHEAD < count:
                begun.append(start(step + AHEAD))
            yield step, begun[step]

    def scores(first, number):
        pairs = [pair(first + step) for step in range(number)]
        made = []
        for step, s in ahead(number, lambda step: dot(ks[pairs[step][1]], qs[pairs[step][0]], NT)):
            i, j = pairs[step]
            at = i * QUERIES + query_lane
            key = key_row + j * KEYS
            seen = (key <= at) & (key >= begin(at))
            e = jnp.exp2(s * (SCALE * LOG2E))
            e = jnp.concatenate(
                [jnp.where(seen, e[:, :QUERIES], 0.0), jnp.where(seen, e[:, QUERIES:], 0.0)],
                axis=1,
            )
            es[first + step] = e
            made.append((i, jnp.sum(e.reshape(KEYS // 8, 8, 2 * QUERIES), axis=0)))
        for i, total in made:
            sums[i] += total

    for_pairs(scores)
    for i in range(QTILES):
        sums[i, 0:1, :] = 1.0 / jnp.sum(sums[i], axis=0, keepdims=True)

    def grads(first, number):
        pairs = [pair(first + step) for step in range(number)]
        made = []
        for step, dp in ahead(number, lambda step: dot(vs[pairs[step][1]], gs[pairs[step][0]], NT)):
            i, j = pairs[step]
            p = es[first + step] * sums[i, 0:1, :]
            ds = (p * (dp - dt[i])).astype(jnp.bfloat16)
            p = p.astype(jnp.bfloat16)
            made.append((i, j, dot(p, gs[i]), dot(ds, qs[i]), dot(kt[j], ds)))
        for i, j, dv, dk, dq in made:
            dvs[j] += dv
            dks[j] += dk
            dqt[i] += dq

    for_pairs(grads)
    for tile in range(KTILES):
        dk = dks[tile] * SCALE
        keep_ref[tile] = jnp.where(core == 0, dk, dvs[tile]).astype(jnp.bfloat16)
        ks[tile] = jnp.where(core == 0, dvs[tile], dk).astype(jnp.bfloat16)
    for src, places in pieces():
        rows = [ks[at // KEYS, at % KEYS : at % KEYS + 16, :] for at in places]
        rows = dot(swap, jnp.concatenate(rows, axis=0)).astype(jnp.bfloat16)
        give_ref[src] = rows.reshape(16, 16, D)


def unsort_kernel(dqt, keep_ref, back_ref, dqs):
    for i in range(QTILES):
        dqs[i] = jnp.transpose(dqt[i] * SCALE).astype(jnp.bfloat16)
    swap = swap_matrix(4)
    for src, places in pieces():
        heads = [
            jnp.concatenate(
                [
                    dqs[at // QUERIES, at % QUERIES + h * QUERIES : at % QUERIES + h * QUERIES + 16]
                    for at in places
                ],
                axis=0,
            )
            for h in range(2)
        ]
        both = dot(swap, jnp.concatenate(heads, axis=1)).astype(jnp.bfloat16)
        back_ref[src, 0:16, :] = both[:, :D].reshape(16, 16, D)
        back_ref[src, 16:32, :] = both[:, D:].reshape(16, 16, D)
        rows = [keep_ref[at // KEYS, at % KEYS : at % KEYS + 16, :] for at in places]
        rows = dot(swap, jnp.concatenate(rows, axis=0)).astype(jnp.bfloat16)
        back_ref[src, 32:48, :] = rows.reshape(16, 16, D)


def add_kernel(mine_ref, other_ref, out_ref):
    total = mine_ref[...].astype(jnp.float32) + other_ref[...].astype(jnp.float32)
    out_ref[...] = total.astype(jnp.bfloat16)


def unpack_kernel(slot_ref, back_ref, q_hbm, k_hbm, v_hbm, qs, ks, vs, sent):
    plan = jnp.transpose(plan_matrix(slot_ref)).astype(jnp.bfloat16)
    both = jnp.concatenate([plan, plan], axis=1)
    copies = []
    for core, out in ((0, ks), (1, vs)):
        for b in range(4):
            rows = jnp.concatenate(
                [
                    back_ref[:, core, :, b, high, 32:48, :].reshape(ROWS, D)
                    for high in range(2)
                ],
                axis=0,
            )
            out[:, b * D : (b + 1) * D] = dot(both, rows).astype(jnp.bfloat16)
        far = (k_hbm, v_hbm)[core]
        copies.append(pltpu.make_async_copy(out, far, sent.at[4 + core]))
        copies[-1].start()
    for b in range(4):
        for head in range(8):
            high, core, h = head // 4, (head // 2) % 2, head % 2
            rows = back_ref[:, core, :, b, high, h * 16 : h * 16 + 16, :].reshape(ROWS, D)
            qs[b, :, head * D : (head + 1) * D] = dot(plan, rows).astype(jnp.bfloat16)
        far = q_hbm.at[:, pl.ds(b * 8 * D, 8 * D)]
        copies.append(pltpu.make_async_copy(qs.at[b], far, sent.at[b]))
        copies[-1].start()
    for copy in copies:
        copy.wait()


def swapped(array):
    return lax.ppermute(array, "dp", [(i, i ^ 1) for i in range(8)])


def vmem(count):
    return [pl.BlockSpec(memory_space=pltpu.VMEM)] * count


SMEM = pl.BlockSpec(memory_space=pltpu.SMEM)
PARAMS = pltpu.CompilerParams(vmem_limit_bytes=VMEM)
WIDE = pltpu.CompilerParams(vmem_limit_bytes=42 * 1024 * 1024)


def cost(flops, size):
    return pl.CostEstimate(flops=flops, bytes_accessed=size, transcendentals=0)


def take(recv):
    return pl.pallas_call(
        take_kernel,
        grid=(4,),
        in_specs=[pl.BlockSpec((32, 16, D), lambda i: (i, 4, 0))],
        out_specs=pl.BlockSpec((32, 16, D), lambda i: (i, 0, 0)),
        out_shape=jax.ShapeDtypeStruct((128, 16, D), jnp.bfloat16),
        compiler_params=PARAMS,
        name="take",
    )(recv)


def sort(info, recv):
    bf, f32 = jnp.bfloat16, jnp.float32
    return pl.pallas_call(
        sort_kernel,
        in_specs=[SMEM] + vmem(1),
        out_specs=vmem(3),
        out_shape=[
            jax.ShapeDtypeStruct((QTILES, 2 * QUERIES, D), bf),
            jax.ShapeDtypeStruct((QTILES, 2 * QUERIES, D), bf),
            jax.ShapeDtypeStruct((QTILES, 1, 2 * QUERIES), f32),
        ],
        scratch_shapes=[pltpu.VMEM((TOKENS, D), bf)],
        compiler_params=PARAMS,
        cost_estimate=cost(10**9, 6 * 10**6),
        name="sort",
    )(info, recv)


def attention(info, near, far, mine, other, q, g, delta):
    bf, f32 = jnp.bfloat16, jnp.float32
    most = sum(i * QUERIES // KEYS + 1 for i in range(QTILES))
    kept = max(pl.cdiv(most, UNROLL) * UNROLL, most + TAIL)
    return pl.pallas_call(
        attention_kernel,
        in_specs=[SMEM] * 3 + vmem(5),
        out_specs=vmem(3),
        out_shape=[
            jax.ShapeDtypeStruct((QTILES, D, 2 * QUERIES), f32),
            jax.ShapeDtypeStruct((KTILES, KEYS, D), bf),
            jax.ShapeDtypeStruct((128, 16, D), bf),
        ],
        scratch_shapes=[
            pltpu.VMEM((KTILES, KEYS, D), bf),
            pltpu.VMEM((KTILES, KEYS, D), bf),
            pltpu.VMEM((KTILES, D, KEYS), bf),
            pltpu.VMEM((kept, KEYS, 2 * QUERIES), f32),
            pltpu.VMEM((KTILES, KEYS, D), f32),
            pltpu.VMEM((KTILES, KEYS, D), f32),
            pltpu.VMEM((QTILES, 8, 2 * QUERIES), f32),
            pltpu.SMEM((2, most + UNROLL + TAIL), jnp.int32),
        ],
        compiler_params=WIDE,
        cost_estimate=cost(4 * 10**9, 10**7),
        name="attention",
    )(info, near, far, mine, other, q, g, delta)


def unsort(dq, keep):
    return pl.pallas_call(
        unsort_kernel,
        in_specs=vmem(2),
        out_specs=vmem(1)[0],
        out_shape=jax.ShapeDtypeStruct((128, 48, D), jnp.bfloat16),
        scratch_shapes=[pltpu.VMEM((QTILES, 2 * QUERIES, D), jnp.bfloat16)],
        compiler_params=PARAMS,
        cost_estimate=cost(10**9, 4 * 10**6),
        name="unsort",
    )(dq, keep)


def add(back, other):
    part = pl.BlockSpec((32, 16, D), lambda i: (i, 0, 0))
    third = pl.BlockSpec((32, 16, D), lambda i: (i, 2, 0))
    return pl.pallas_call(
        add_kernel,
        grid=(4,),
        in_specs=[third, part],
        out_specs=third,
        out_shape=jax.ShapeDtypeStruct((128, 48, D), jnp.bfloat16),
        input_output_aliases={0: 0},
        compiler_params=PARAMS,
        name="add",
    )(back, other)


HBM = pl.BlockSpec(memory_space=pltpu.HBM)


def pack(slot, q, o, g, k, v):
    bf = jnp.bfloat16
    return pl.pallas_call(
        pack_kernel,
        in_specs=[HBM] * 6,
        out_specs=vmem(1)[0],
        out_shape=jax.ShapeDtypeStruct((*CUT, 88, D), bf),
        scratch_shapes=[pltpu.VMEM((1, ROWS), jnp.int32)]
        + [pltpu.VMEM((4, ROWS, 8 * D), bf)] * 3
        + [pltpu.VMEM((ROWS, 4 * D), bf)] * 2
        + [pltpu.SemaphoreType.DMA((15,))],
        compiler_params=pltpu.CompilerParams(vmem_limit_bytes=32 * 1024 * 1024),
        name="pack",
    )(slot, q, o, g, k, v)


def unpack(slot, back):
    bf = jnp.bfloat16
    return pl.pallas_call(
        unpack_kernel,
        in_specs=vmem(2),
        out_specs=[HBM] * 3,
        out_shape=[
            jax.ShapeDtypeStruct((ROWS, 32 * D), bf),
            jax.ShapeDtypeStruct((ROWS, 4 * D), bf),
            jax.ShapeDtypeStruct((ROWS, 4 * D), bf),
        ],
        scratch_shapes=[
            pltpu.VMEM((4, ROWS, 8 * D), bf),
            pltpu.VMEM((ROWS, 4 * D), bf),
            pltpu.VMEM((ROWS, 4 * D), bf),
            pltpu.SemaphoreType.DMA((6,)),
        ],
        compiler_params=PARAMS,
        name="unpack",
    )(slot, back)


def per_device(queries, keys, values, attn_out, out_grad, send_slot, proof_length_list):
    core = lax.axis_index("dp") & 1
    ctx = lax.axis_index("ctx")
    info = jnp.stack([core, (ctx & 1) * 2 + core, ctx >> 3 == core]).astype(jnp.int32)
    lengths = swapped(proof_length_list)

    far = [
        pltpu.with_memory_space_constraint(array, pltpu.HBM)
        for array in (send_slot, queries, attn_out, out_grad, keys, values)
    ]
    send, lengths = lax.optimization_barrier((pack(*far), lengths))
    recv = lax.all_to_all(
        send.reshape(128, 88, D), ("dp", "ctx"), split_axis=0, concat_axis=0, tiled=True
    )
    mine = take(recv)
    other = swapped(mine)
    q, g, delta = sort(info, recv)
    dq, keep, give = attention(info, proof_length_list, lengths, mine, other, q, g, delta)
    back = add(unsort(dq, keep), swapped(give))
    back = lax.all_to_all(back, ("dp", "ctx"), split_axis=0, concat_axis=0, tiled=True)
    return unpack(send_slot, back.reshape(*CUT, 48, D))


def solution(mesh):
    rows = P(("dp", "ctx"), None)
    return jax.shard_map(
        per_device,
        mesh=mesh,
        in_specs=(rows, rows, rows, rows, rows, rows, P("dp", None)),
        out_specs=(rows, rows, rows),
        check_vma=False,
    )
```
